256 devices in a mesh: dp: 64 (over x, z, y_hi), mp: 4 (over y_lo, core).
Axes of the slice: x: 4, y: 4 (y_hi: 2, y_lo: 2; y = y_hi * 2 + y_lo), z: 8, core: 2. Of those that a mesh axis runs over, the one named last changes fastest.
Arguments:
- patches: bfloat16 [131072, 1152], P('dp', 'mp')
- counts: int32 [128], P('dp'), may hold values from 256 to 1024, as said below
- pair_ids: int32 [128], P('dp'), may hold values from 0 to 127, each once
- inner_weight: bfloat16 [1152, 4304], P(None, 'mp'), may hold values from -0.1875 to 0.1875
- outer_weight: bfloat16 [4304, 1152], P('mp'), may hold values from -0.09375 to 0.09375
- text_embed: bfloat16 [128, 1152], P('dp', 'mp')
- log_scale: float32 [1], replicated, may hold values from 1.5 to 2.5
- logit_bias: float32 [1], replicated, may hold values from -5 to -2
Outputs:
- image_loss: float32 [128], P('dp')
- emb_grad: float32 [128, 1152], P('dp', 'mp')
- text_grad: float32 [128, 1152], P('dp', 'mp')
The draws below stay inside these ranges and needn't reach their ends.
Inputs may be any that keep to these rules, and one draw needn't show every extreme that they name: `counts`: in every draw the images of some shard fill all of its 2048 rows. `pair_ids`: each text index appears once.
All inputs are finite; a program needn't handle non-finite values.
Results may differ from the reference program's by a relative error of at most 0.0036.
Values may be sent and summed in bfloat16 or wider, within the bound.
A program may use at most 128 MiB of HBM per device.

```python
import math
import jax
import jax.numpy as jnp
from jax import lax

D = 1152
FF = 4304
IMG_DEV = 2
MAXP = 1024
MINP = 256
ROWS_DEV = 2048
ROWS = 131072
B = 128
N_DP = 64


def count_values(key):
    key = jax.random.fold_in(key, 11)
    keys = jax.random.split(key, 3)
    shard_total = B // IMG_DEV
    values = jax.random.randint(keys[0], (B,), MINP, MAXP + 1)
    full_shard = jax.random.randint(keys[1], (), 0, shard_total)
    other_shard = (full_shard + 1 + jax.random.randint(keys[2], (), 0, max(shard_total - 1, 1))) % shard_total
    position = jnp.arange(B)
    values = jnp.where(position == other_shard * IMG_DEV, MINP, values)
    values = jnp.where(position // IMG_DEV == full_shard, MAXP, values)
    return values.astype(jnp.int32)


def scaled_table(key, rows, columns, row_low, row_high, column_low, column_high, extra):
    keys = jax.random.split(key, 3)
    row_scale = jnp.exp(jax.random.uniform(keys[0], (rows, 1), jnp.float32, math.log(row_low), math.log(row_high)))
    column_scale = jnp.exp(jax.random.uniform(keys[1], (1, columns), jnp.float32, math.log(column_low), math.log(column_high)))
    values = jax.random.normal(keys[2], (rows, columns), jnp.float32) + extra
    return values * row_scale * column_scale


def draw_patches(key, part):
    image_counts = count_values(key)
    key = jax.random.fold_in(key, 5)
    keys = jax.random.split(key, 2)
    shard_total = B // IMG_DEV
    image_part = jax.random.normal(keys[1], (B, D), jnp.float32)
    row_ends = jnp.cumsum(image_counts.reshape(shard_total, IMG_DEV), axis=1)
    row_ids = jnp.arange(ROWS_DEV, dtype=jnp.int32)
    passed = (row_ids[None, :, None] >= row_ends[:, None, :]).astype(jnp.int32)
    slot = jnp.minimum(jnp.sum(passed, axis=2), IMG_DEV - 1)
    image_index = (jnp.arange(shard_total, dtype=jnp.int32)[:, None] * IMG_DEV + slot).reshape(ROWS)
    per_row = image_part[image_index]
    return scaled_table(keys[0], ROWS, D, 0.3, 3.0, 0.5, 5.0, per_row).astype(jnp.bfloat16)


def draw_text_embed(key, part):
    key = jax.random.fold_in(key, 7)
    return (0.03 * scaled_table(key, B, D, 1.0, 10.0, 0.5, 2.0, 0.0)).astype(jnp.bfloat16)


def draw_counts(key, part):
    return count_values(key)


def level_of(stream_key, shape, pieces, low, high):
    def one(axis_at, blocks):
        steps = jax.random.uniform(jax.random.fold_in(jax.random.fold_in(stream_key, 6), axis_at), (blocks,), jnp.float32, low / len(pieces), high / len(pieces))
        return jnp.repeat(jnp.exp(steps), shape[axis_at] // blocks).reshape((-1,) + (1,) * (len(shape) - axis_at - 1))

    gain = one(*pieces[0])
    for cut in pieces[1:]:
        gain = gain * one(*cut)
    return gain


def centred(own_key, shape, deviation, most, pieces=(), held_as=jnp.bfloat16):
    result = jax.random.normal(own_key, shape, jnp.float32) * deviation
    if len(pieces) > 0:
        result = level_of(own_key, shape, pieces, -0.22, 0.18) * result
    return jnp.clip(result, min=-most, max=most).astype(held_as)


def setup_inputs(seed: int = 0) -> dict:
    seeds = jax.random.split(jax.random.key(seed), 9)
    patches = draw_patches(jax.random.fold_in(seeds[8], 71), 0)
    counts = draw_counts(jax.random.fold_in(seeds[8], 71), 0)
    pair_ids = jax.random.permutation(seeds[2], B).astype(jnp.int32)
    inner_weight = centred(seeds[3], (D, FF), D ** -0.5, 0.1875, ((1, 4),))
    outer_weight = centred(seeds[4], (FF, D), FF ** -0.5, 0.09375, ((0, 4),))
    text_embed = draw_text_embed(jax.random.fold_in(seeds[8], 71), 0)
    log_scale = jnp.clip(jax.random.uniform(seeds[6], (1,), jnp.float32, 1.5, 2.5), 1.5, 2.5)
    logit_bias = jnp.clip(jax.random.uniform(seeds[7], (1,), jnp.float32, -5.0, -2.0), -5.0, -2.0)
    return {"patches": patches, "counts": counts, "pair_ids": pair_ids, "inner_weight": inner_weight, "outer_weight": outer_weight, "text_embed": text_embed, "log_scale": log_scale, "logit_bias": logit_bias}


epsilon = 1e-06

def layer_norm(values):
    centre = lax.optimization_barrier(jnp.mean(values, axis=-1, keepdims=True))
    shifted = values - centre
    spread = lax.optimization_barrier(jnp.mean(shifted * shifted, axis=-1, keepdims=True))
    return shifted * lax.rsqrt(spread + epsilon)

def reference(patches, counts, pair_ids, inner_weight, outer_weight, text_embed, log_scale, logit_bias):
    shards = patches.reshape(N_DP, ROWS_DEV, D)
    lengths = counts.reshape(N_DP, IMG_DEV)

    def image_tower(item):
        patch_rows, shard_counts = item
        normed = layer_norm(patch_rows.astype(jnp.float32)).astype(jnp.bfloat16)
        hidden = jax.nn.gelu(jnp.dot(normed, inner_weight, preferred_element_type=jnp.float32), approximate=True).astype(jnp.bfloat16)
        updated = patch_rows.astype(jnp.float32) + jnp.dot(hidden, outer_weight, preferred_element_type=jnp.float32)
        final_rows = layer_norm(updated)
        row_ends = jnp.cumsum(shard_counts).astype(jnp.int32)
        row_starts = row_ends - shard_counts.astype(jnp.int32)
        row_ids = jnp.arange(ROWS_DEV, dtype=jnp.int32)
        member = ((row_ids[None, :] >= row_starts[:, None]) & (row_ids[None, :] < row_ends[:, None])).astype(jnp.float32)
        summed = jnp.dot(member, final_rows, precision=lax.Precision.HIGHEST)
        return summed / shard_counts[:, None].astype(jnp.float32)
    pooled = lax.map(image_tower, (shards, lengths)).reshape(B, D)
    image_norm = lax.rsqrt(lax.optimization_barrier(jnp.sum(pooled * pooled, axis=1)) + epsilon)
    unit_image = pooled * image_norm[:, None]
    image_wire = unit_image.astype(jnp.bfloat16)
    text_values = text_embed.astype(jnp.float32)
    text_norm = lax.rsqrt(lax.optimization_barrier(jnp.sum(text_values * text_values, axis=1)) + epsilon)
    text_unit = text_values * text_norm[:, None]
    text_wire = text_unit.astype(jnp.bfloat16)
    logit_scale = jnp.exp(log_scale[0])
    logits = logit_scale * jnp.dot(image_wire, text_wire.T, preferred_element_type=jnp.float32) + logit_bias[0]
    text_ids = jnp.arange(B, dtype=jnp.int32)
    labels = jnp.where(pair_ids[:, None] == text_ids[None, :], 1.0, -1.0).astype(jnp.float32)
    image_loss = lax.optimization_barrier(jnp.sum(jax.nn.softplus(-labels * logits), axis=1))
    slopes = -labels * jax.nn.sigmoid(-labels * logits)
    image_dir = logit_scale * jnp.dot(slopes, text_wire.astype(jnp.float32), precision=lax.Precision.HIGHEST)
    text_dir = logit_scale * jnp.dot(slopes.T, image_wire.astype(jnp.float32), precision=lax.Precision.HIGHEST)
    emb_grad = (image_dir - unit_image * lax.optimization_barrier(jnp.sum(unit_image * image_dir, axis=1, keepdims=True))) * image_norm[:, None]
    text_grad = (text_dir - text_unit * lax.optimization_barrier(jnp.sum(text_unit * text_dir, axis=1, keepdims=True))) * text_norm[:, None]
    return (image_loss, emb_grad, text_grad)
```

```python
import functools

import jax
import jax.numpy as jnp
from jax import lax
from jax.experimental import pallas as pl
from jax.experimental.pallas import tpu as pltpu
from jax.sharding import PartitionSpec as P

MESH = pl.DeviceIdType.MESH
epsilon = 1e-06
D = 1152
DL = 288
F32, BF16 = jnp.float32, jnp.bfloat16


def layer_norm(values):
    centre = jnp.mean(values, axis=-1, keepdims=True)
    shifted = values - centre
    spread = jnp.mean(shifted * shifted, axis=-1, keepdims=True)
    return shifted * lax.rsqrt(spread + epsilon)


def expand_rows(normed, weights):
    return jax.nn.gelu(
        jnp.dot(normed, weights, preferred_element_type=jnp.float32), approximate=True
    )


def coords():
    dp, mp = lax.axis_index("dp"), lax.axis_index("mp")
    return dp // 16, (dp // 2) % 8, dp % 2, mp


def dp_of(x, z, yh):
    return x * 16 + z * 2 + yh


def tail_peers():
    x, z, yh, mp = coords()
    dp = dp_of(x, z, yh)
    group = [(dp, (mp + k) % 4) for k in range(1, 4)]
    line = [(dp_of(x, (z + k) % 8, yh), mp) for k in range(1, 8)]
    plane = [(dp_of((x + k // 2) % 4, z, (yh + k) % 2), mp) for k in range(1, 8)]
    return group, line, plane


def tail_body(
    counts_ref, pair_ref, scale_ref, bias_ref, loss_ref, emb_ref, txt_ref,
    sums, rows, packed, msg, dots, group_send, group_recv, line_send, line_recv,
    plane_send, plane_recv, dots_send, dots_recv,
):
    x, z, yh, mp = coords()
    group, line, plane = tail_peers()
    dp = dp_of(x, z, yh)
    slot = (x * 2 + yh) * 8 + z

    copies = []
    for k, peer in enumerate(group):
        copies.append(pltpu.make_async_remote_copy(
            src_ref=sums.at[mp], dst_ref=sums.at[mp], send_sem=group_send.at[k],
            recv_sem=group_recv.at[k], device_id=peer, device_id_type=MESH))
        copies[-1].start()
    for copy in copies:
        copy.wait_recv()
    total = ((sums[0] + sums[1]) + sums[2]) + sums[3]
    row = lax.broadcasted_iota(jnp.int32, (8, 1), 0)
    count = jnp.where(row == 0, counts_ref[0], jnp.where(row == 1, counts_ref[1], 1)).astype(F32)
    values = total / count
    norm = lax.rsqrt(jnp.sum(values * values, axis=1, keepdims=True) + epsilon)
    unit = values * norm
    rows[:, :D] = unit
    rows[:, D:] = jnp.zeros((8, rows.shape[1] - D), F32)
    lane = lax.broadcasted_iota(jnp.int32, (4, 128), 1)
    units = []
    for b in range(3):
        block = jnp.zeros((4, 128), F32)
        for k in range(4):
            block = jnp.where(mp == k, rows[0:4, DL * k + 128 * b: DL * k + 128 * b + 128], block)
        if b == 2:
            block = jnp.where(lane < DL - 256, block, 0.0)
        units.append(block)
        packed[4 * b:4 * b + 4, :] = block
    line4 = lax.broadcasted_iota(jnp.int32, (4, 128), 0)
    packed[12:16, :] = jnp.where(
        line4 == 0, pair_ref[0].astype(F32), jnp.where(line4 == 1, pair_ref[1].astype(F32), 0.0))
    msg[slot] = packed[...].astype(BF16)

    sends = []
    for k, peer in enumerate(line):
        sends.append(pltpu.make_async_remote_copy(
            src_ref=msg.at[slot], dst_ref=msg.at[slot], send_sem=line_send.at[k],
            recv_sem=line_recv.at[k], device_id=peer, device_id_type=MESH))
        sends[-1].start()
    row16 = lax.broadcasted_iota(jnp.int32, (16, 128), 0)
    lane16 = lax.broadcasted_iota(jnp.int32, (16, 128), 1)
    for b in range(3):
        wire = units[b].astype(BF16).astype(F32)
        packed[0:4, :] = wire
        packed[4:8, :] = units[b] - wire
        packed[8:16, :] = jnp.zeros((8, 128), F32)
        left = packed[...]
        if b == 0:
            left = jnp.where((row16 == 8) & (lane16 == 0), 1.0, left)
        rows_b = left.astype(BF16)
        lefts = [rows_b] if b == 0 else lefts + [rows_b]
    left = jnp.concatenate(lefts, axis=0)
    for copy in sends:
        copy.wait_recv()
    first = (x * 2 + yh) * 8
    for k, peer in enumerate(plane):
        sends.append(pltpu.make_async_remote_copy(
            src_ref=msg.at[pl.ds(first, 8)], dst_ref=msg.at[pl.ds(first, 8)], send_sem=plane_send.at[k],
            recv_sem=plane_recv.at[k], device_id=peer, device_id_type=MESH))
        sends[-1].start()
    for copy in sends[7:]:
        copy.wait_recv()
    everyone = msg[...].reshape(1024, 128)
    prod = lax.dot_general(left, everyone, (((1,), (1,)), ((), ())), preferred_element_type=F32)
    pairs = pltpu.roll(prod[0:16], 1024 - 12, 1)[8:9]
    part = prod[0:16] + pltpu.roll(prod[16:32], 1024 - 4, 1) + pltpu.roll(prod[32:48], 1024 - 8, 1)
    dots[mp] = part[0:8]
    swaps = []
    for k, peer in enumerate(group):
        swaps.append(pltpu.make_async_remote_copy(
            src_ref=dots.at[mp], dst_ref=dots.at[mp], send_sem=dots_send.at[k],
            recv_sem=dots_recv.at[k], device_id=peer, device_id_type=MESH))
        swaps[-1].start()
    for copy in swaps:
        copy.wait_recv()
    dot = ((dots[0] + dots[1]) + dots[2]) + dots[3]
    column = lax.broadcasted_iota(jnp.int32, (8, 1024), 1)
    place, kind = column // 16, column % 16
    shard = (place // 16) * 16 + (place % 8) * 2 + (place // 8) % 2
    row8 = lax.broadcasted_iota(jnp.int32, (8, 1024), 0)
    own_pair = jnp.where(row8 == 0, pair_ref[0], pair_ref[1])
    all_pair = jnp.broadcast_to(pairs, (8, 1024)).astype(jnp.int32)
    wanted = jnp.where(row8 < 2, own_pair, all_pair)
    match = wanted == jnp.where(row8 < 2, shard * 2 + kind - 2, dp * 2 + row8 - 2)
    valid = ((row8 < 2) & ((kind == 2) | (kind == 3))) | ((row8 >= 2) & (row8 < 4) & (kind < 2))
    scale = jnp.exp(jnp.full((8, 1024), scale_ref[0], F32))
    label = jnp.where(match, 1.0, -1.0)
    turned = -label * (scale * dot + bias_ref[0])
    small = jnp.exp(-jnp.abs(turned))
    soft = jnp.where(valid, jnp.maximum(turned, 0.0) + jnp.log1p(small), 0.0)
    sigmoid = jnp.where(turned >= 0, 1.0, small) / (1.0 + small)
    slope = jnp.where(valid, -label * sigmoid, 0.0)
    loss = jnp.sum(soft, axis=1, keepdims=True)
    whole = dot + pltpu.roll(dot, 4, 0)
    proj = jnp.sum(scale * slope * whole, axis=1, keepdims=True)[0:4]
    high = slope.astype(BF16)
    rest = slope - high.astype(F32)
    mid = rest.astype(BF16)
    low = (rest - mid.astype(F32)).astype(BF16)
    stack = jnp.concatenate([high.astype(F32), mid.astype(F32), low.astype(F32)], axis=0)
    stack = jnp.concatenate([stack, pltpu.roll(stack, 4, 1), pltpu.roll(stack, 8, 1)], axis=0).astype(BF16)
    dirs = jnp.dot(stack, everyone, preferred_element_type=F32)
    for b in range(3):
        own = dirs[24 * b:24 * b + 24]
        direction = (own[0:8] + (own[8:16] + own[16:24]))[0:4] * scale[0:4, 0:128]
        grad = (direction - units[b] * proj) * norm[0:4]
        width = 128 if b < 2 else DL - 256
        emb_ref[:, 128 * b:128 * b + width] = grad[0:2, :width]
        txt_ref[:, 128 * b:128 * b + width] = grad[2:4, :width]
    loss_ref[...] = jnp.broadcast_to(loss[0:2], (2, 128))
    for copy in copies + sends + swaps:
        copy.wait_send()


def tail_kernel(sum_ref, text_ref, counts_ref, pair_ref, scale_ref, bias_ref, loss_ref, emb_ref, txt_ref, *scratch):
    sums = scratch[0]
    mp = lax.axis_index("mp")
    barrier = pltpu.get_barrier_semaphore()
    group, line, plane = tail_peers()
    for peer in group + line + plane:
        pl.semaphore_signal(barrier, inc=1, device_id=peer, device_id_type=MESH)
    sums[mp] = jnp.zeros((8, D), F32)
    sums[mp, 0:2, :] = sum_ref[...]
    for k in range(4):
        @pl.when(mp == k)
        def _():
            sums[k, 2:4, DL * k:DL * k + DL] = text_ref[...].astype(F32)
    pl.semaphore_wait(barrier, 17)
    tail_body(counts_ref, pair_ref, scale_ref, bias_ref, loss_ref, emb_ref, txt_ref, *scratch)


def tail_scratch():
    dma = pltpu.SemaphoreType.DMA
    return [
        pltpu.VMEM((4, 8, D), F32),
        pltpu.VMEM((8, D + 128), F32),
        pltpu.VMEM((16, 128), F32),
        pltpu.VMEM((64, 16, 128), BF16),
        pltpu.VMEM((4, 8, 1024), F32),
        dma((3,)), dma((3,)), dma((7,)), dma((7,)), dma((7,)), dma((7,)), dma((3,)), dma((3,)),
    ]


def tail(sums, text, counts, pairs, log_scale, logit_bias):
    vmem, smem = pl.BlockSpec(memory_space=pltpu.VMEM), pl.BlockSpec(memory_space=pltpu.SMEM)
    loss, emb, txt = pl.pallas_call(
        tail_kernel,
        out_shape=(
            jax.ShapeDtypeStruct((2, 128), F32),
            jax.ShapeDtypeStruct((2, DL), F32),
            jax.ShapeDtypeStruct((2, DL), F32),
        ),
        in_specs=[vmem, vmem, smem, smem, smem, smem],
        out_specs=(vmem, vmem, vmem),
        scratch_shapes=tail_scratch(),
        compiler_params=pltpu.CompilerParams(collective_id=1, has_side_effects=True),
        name="tail",
    )(sums, text, counts, pairs, log_scale, logit_bias)
    return loss[:, 0], emb, txt


def shards(
    patches, counts, pair_ids, inner_weight, outer_weight, text_embed, log_scale, logit_bias
):
    group_size = lax.axis_size("mp")
    shard_rows = patches.shape[0]
    own_count = shard_rows // group_size
    row_first = lax.axis_index("mp") * own_count
    full_rows = lax.all_gather(patches, "mp", axis=1, tiled=True)
    normed = layer_norm(full_rows.astype(jnp.float32)).astype(jnp.bfloat16)
    hidden = expand_rows(normed, inner_weight).astype(jnp.bfloat16)
    mixed_rows = lax.psum_scatter(
        jnp.dot(hidden, outer_weight, preferred_element_type=jnp.float32),
        "mp",
        scatter_dimension=0,
        tiled=True,
    )
    own_rows = lax.dynamic_slice_in_dim(full_rows, row_first, own_count, 0)
    updated = own_rows.astype(jnp.float32) + mixed_rows
    final_rows = layer_norm(updated)
    row_ends = jnp.cumsum(counts)
    row_starts = row_ends - counts
    row_ids = row_first + jnp.arange(own_count, dtype=jnp.int32)
    member = (
        (row_ids[None, :] >= row_starts[:, None]) & (row_ids[None, :] < row_ends[:, None])
    ).astype(jnp.float32)
    partial_value = jnp.dot(member, final_rows, precision=lax.Precision.HIGHEST)
    return tail(partial_value, text_embed, counts, pair_ids, log_scale, logit_bias)


def solution(mesh):
    placed = (
        P("dp", "mp"),
        P("dp"),
        P("dp"),
        P(None, "mp"),
        P("mp", None),
        P("dp", "mp"),
        P(),
        P(),
    )
    return jax.shard_map(
        shards,
        mesh=mesh,
        in_specs=placed,
        out_specs=(P("dp"), P("dp", "mp"), P("dp", "mp")),
        check_vma=False,
    )
```

```python
import functools

import jax
import jax.numpy as jnp
from jax import lax
from jax.experimental import pallas as pl
from jax.experimental.pallas import tpu as pltpu
from jax.sharding import PartitionSpec as P

MESH = pl.DeviceIdType.MESH
epsilon = 1e-06
D = 1152
DL = 288
F32, BF16 = jnp.float32, jnp.bfloat16


def coords():
    dp, mp = lax.axis_index("dp"), lax.axis_index("mp")
    return dp // 16, (dp // 2) % 8, dp % 2, mp


def dp_of(x, z, yh):
    return x * 16 + z * 2 + yh


def tail_peers():
    x, z, yh, mp = coords()
    dp = dp_of(x, z, yh)
    group = [(dp, (mp + k) % 4) for k in range(1, 4)]
    line = [(dp_of(x, (z + k) % 8, yh), mp) for k in range(1, 8)]
    plane = [(dp_of((x + k // 2) % 4, z, (yh + k) % 2), mp) for k in range(1, 8)]
    return group, line, plane


def tail_body(
    counts_ref, pair_ref, scale_ref, bias_ref, loss_ref, emb_ref, txt_ref,
    sums, rows, packed, msg, dots, group_send, group_recv, line_send, line_recv,
    plane_send, plane_recv, dots_send, dots_recv,
):
    x, z, yh, mp = coords()
    group, line, plane = tail_peers()
    dp = dp_of(x, z, yh)
    slot = (x * 2 + yh) * 8 + z

    copies = []
    for k, peer in enumerate(group):
        copies.append(pltpu.make_async_remote_copy(
            src_ref=sums.at[mp], dst_ref=sums.at[mp], send_sem=group_send.at[k],
            recv_sem=group_recv.at[k], device_id=peer, device_id_type=MESH))
        copies[-1].start()
    for copy in copies:
        copy.wait_recv()
    total = ((sums[0] + sums[1]) + sums[2]) + sums[3]
    row = lax.broadcasted_iota(jnp.int32, (8, 1), 0)
    count = jnp.where(row == 0, counts_ref[0], jnp.where(row == 1, counts_ref[1], 1)).astype(F32)
    values = total / count
    norm = lax.rsqrt(jnp.sum(values * values, axis=1, keepdims=True) + epsilon)
    unit = values * norm
    rows[:, :D] = unit
    rows[:, D:] = jnp.zeros((8, rows.shape[1] - D), F32)
    lane = lax.broadcasted_iota(jnp.int32, (4, 128), 1)
    units = []
    for b in range(3):
        block = jnp.zeros((4, 128), F32)
        for k in range(4):
            block = jnp.where(mp == k, rows[0:4, DL * k + 128 * b: DL * k + 128 * b + 128], block)
        if b == 2:
            block = jnp.where(lane < DL - 256, block, 0.0)
        units.append(block)
        packed[4 * b:4 * b + 4, :] = block
    line4 = lax.broadcasted_iota(jnp.int32, (4, 128), 0)
    packed[12:16, :] = jnp.where(
        line4 == 0, pair_ref[0].astype(F32), jnp.where(line4 == 1, pair_ref[1].astype(F32), 0.0))
    msg[slot] = packed[...].astype(BF16)

    sends = []
    for k, peer in enumerate(line):
        sends.append(pltpu.make_async_remote_copy(
            src_ref=msg.at[slot], dst_ref=msg.at[slot], send_sem=line_send.at[k],
            recv_sem=line_recv.at[k], device_id=peer, device_id_type=MESH))
        sends[-1].start()
    row16 = lax.broadcasted_iota(jnp.int32, (16, 128), 0)
    lane16 = lax.broadcasted_iota(jnp.int32, (16, 128), 1)
    for b in range(3):
        wire = units[b].astype(BF16).astype(F32)
        packed[0:4, :] = wire
        packed[4:8, :] = units[b] - wire
        packed[8:16, :] = jnp.zeros((8, 128), F32)
        left = packed[...]
        if b == 0:
            left = jnp.where((row16 == 8) & (lane16 == 0), 1.0, left)
        rows_b = left.astype(BF16)
        lefts = [rows_b] if b == 0 else lefts + [rows_b]
    left = jnp.concatenate(lefts, axis=0)
    for copy in sends:
        copy.wait_recv()
    first = (x * 2 + yh) * 8
    for k, peer in enumerate(plane):
        sends.append(pltpu.make_async_remote_copy(
            src_ref=msg.at[pl.ds(first, 8)], dst_ref=msg.at[pl.ds(first, 8)], send_sem=plane_send.at[k],
            recv_sem=plane_recv.at[k], device_id=peer, device_id_type=MESH))
        sends[-1].start()
    for copy in sends[7:]:
        copy.wait_recv()
    everyone = msg[...].reshape(1024, 128)
    prod = lax.dot_general(left, everyone, (((1,), (1,)), ((), ())), preferred_element_type=F32)
    pairs = pltpu.roll(prod[0:16], 1024 - 12, 1)[8:9]
    part = prod[0:16] + pltpu.roll(prod[16:32], 1024 - 4, 1) + pltpu.roll(prod[32:48], 1024 - 8, 1)
    dots[mp] = part[0:8]
    swaps = []
    for k, peer in enumerate(group):
        swaps.append(pltpu.make_async_remote_copy(
            src_ref=dots.at[mp], dst_ref=dots.at[mp], send_sem=dots_send.at[k],
            recv_sem=dots_recv.at[k], device_id=peer, device_id_type=MESH))
        swaps[-1].start()
    for copy in swaps:
        copy.wait_recv()
    dot = ((dots[0] + dots[1]) + dots[2]) + dots[3]
    column = lax.broadcasted_iota(jnp.int32, (8, 1024), 1)
    place, kind = column // 16, column % 16
    shard = (place // 16) * 16 + (place % 8) * 2 + (place // 8) % 2
    row8 = lax.broadcasted_iota(jnp.int32, (8, 1024), 0)
    own_pair = jnp.where(row8 == 0, pair_ref[0], pair_ref[1])
    all_pair = jnp.broadcast_to(pairs, (8, 1024)).astype(jnp.int32)
    wanted = jnp.where(row8 < 2, own_pair, all_pair)
    match = wanted == jnp.where(row8 < 2, shard * 2 + kind - 2, dp * 2 + row8 - 2)
    valid = ((row8 < 2) & ((kind == 2) | (kind == 3))) | ((row8 >= 2) & (row8 < 4) & (kind < 2))
    scale = jnp.exp(jnp.full((8, 1024), scale_ref[0], F32))
    label = jnp.where(match, 1.0, -1.0)
    turned = -label * (scale * dot + bias_ref[0])
    small = jnp.exp(-jnp.abs(turned))
    soft = jnp.where(valid, jnp.maximum(turned, 0.0) + jnp.log1p(small), 0.0)
    sigmoid = jnp.where(turned >= 0, 1.0, small) / (1.0 + small)
    slope = jnp.where(valid, -label * sigmoid, 0.0)
    loss = jnp.sum(soft, axis=1, keepdims=True)
    whole = dot + pltpu.roll(dot, 4, 0)
    proj = jnp.sum(scale * slope * whole, axis=1, keepdims=True)[0:4]
    high = slope.astype(BF16)
    rest = slope - high.astype(F32)
    mid = rest.astype(BF16)
    low = (rest - mid.astype(F32)).astype(BF16)
    stack = jnp.concatenate([high.astype(F32), mid.astype(F32), low.astype(F32)], axis=0)
    stack = jnp.concatenate([stack, pltpu.roll(stack, 4, 1), pltpu.roll(stack, 8, 1)], axis=0).astype(BF16)
    dirs = jnp.dot(stack, everyone, preferred_element_type=F32)
    for b in range(3):
        own = dirs[24 * b:24 * b + 24]
        direction = (own[0:8] + (own[8:16] + own[16:24]))[0:4] * scale[0:4, 0:128]
        grad = (direction - units[b] * proj) * norm[0:4]
        width = 128 if b < 2 else DL - 256
        emb_ref[:, 128 * b:128 * b + width] = grad[0:2, :width]
        txt_ref[:, 128 * b:128 * b + width] = grad[2:4, :width]
    loss_ref[...] = jnp.broadcast_to(loss[0:2], (2, 128))
    for copy in copies + sends + swaps:
        copy.wait_send()


def tail_kernel(sum_ref, text_ref, counts_ref, pair_ref, scale_ref, bias_ref, loss_ref, emb_ref, txt_ref, *scratch):
    sums = scratch[0]
    mp = lax.axis_index("mp")
    barrier = pltpu.get_barrier_semaphore()
    group, line, plane = tail_peers()
    for peer in group + line + plane:
        pl.semaphore_signal(barrier, inc=1, device_id=peer, device_id_type=MESH)
    sums[mp] = jnp.zeros((8, D), F32)
    sums[mp, 0:2, :] = sum_ref[...]
    for k in range(4):
        @pl.when(mp == k)
        def _():
            sums[k, 2:4, DL * k:DL * k + DL] = text_ref[...].astype(F32)
    pl.semaphore_wait(barrier, 17)
    tail_body(counts_ref, pair_ref, scale_ref, bias_ref, loss_ref, emb_ref, txt_ref, *scratch)


def tail_scratch():
    dma = pltpu.SemaphoreType.DMA
    return [
        pltpu.VMEM((4, 8, D), F32),
        pltpu.VMEM((8, D + 128), F32),
        pltpu.VMEM((16, 128), F32),
        pltpu.VMEM((64, 16, 128), BF16),
        pltpu.VMEM((4, 8, 1024), F32),
        dma((3,)), dma((3,)), dma((7,)), dma((7,)), dma((7,)), dma((7,)), dma((3,)), dma((3,)),
    ]


def tail(sums, text, counts, pairs, log_scale, logit_bias):
    vmem, smem = pl.BlockSpec(memory_space=pltpu.VMEM), pl.BlockSpec(memory_space=pltpu.SMEM)
    loss, emb, txt = pl.pallas_call(
        tail_kernel,
        out_shape=(
            jax.ShapeDtypeStruct((2, 128), F32),
            jax.ShapeDtypeStruct((2, DL), F32),
            jax.ShapeDtypeStruct((2, DL), F32),
        ),
        in_specs=[vmem, vmem, smem, smem, smem, smem],
        out_specs=(vmem, vmem, vmem),
        scratch_shapes=tail_scratch(),
        compiler_params=pltpu.CompilerParams(collective_id=1, has_side_effects=True),
        name="tail",
    )(sums, text, counts, pairs, log_scale, logit_bias)
    return loss[:, 0], emb, txt


ROWS = 512
MAIN = 1024
TAIL = 64
LINK = {}
for _s in range(10):
    for _k in range(2):
        LINK[_s, _k] = "hi" if _s < 5 else ("hi", "lo")[_k]


def stage_rows(stage):
    local = stage % 5
    return (0, 16) if local == 0 else (128 + 256 * (local - 1), 32)


def main_peers():
    x, z, yh, mp = coords()
    dp = dp_of(x, z, yh)
    return dict(
        core=(dp, mp + 1 - 2 * (mp % 2)),
        lo=(dp, (mp + 2) % 4),
        cross=(dp, 3 - mp),
        hi=(dp + 1 - 2 * (dp % 2), (mp + 2) % 4),
        xp=(dp_of((x + 1) % 4, z, yh), mp),
        xm=(dp_of((x + 3) % 4, z, yh), mp),
        zp=(dp_of(x, (z + 1) % 8, yh), mp),
        zm=(dp_of(x, (z + 7) % 8, yh), mp),
    )


def gelu(u):
    inner = u * (0.7978845608028654 + 0.035677408136300125 * (u * u))
    half = 0.5 * u
    return half + half * jnp.tanh(inner)


def main_kernel(
    patch_ref, inner_ref, outer_ref, tail_ref, counts_ref, out_ref,
    w1_own, w2_own, w1_oth, w2_oth, xin, xres, xn, acc, hid, hid_oth, part_out, part_in,
    load_sem, own_sem, patch_send, patch_recv, norm_send, norm_recv, y_send, y_recv,
    side_send, side_recv, part_send, part_recv,
):
    x, z, yh, mp = coords()
    dp = dp_of(x, z, yh)
    core = mp % 2
    colour = [(x + 2 * z) % 4, (2 * x + z) % 4]
    peers = main_peers()
    barrier = pltpu.get_barrier_semaphore()
    for peer in peers.values():
        pl.semaphore_signal(barrier, inc=1, device_id=peer, device_id_type=MESH)
    loads = [
        pltpu.make_async_copy(inner_ref.at[:, pl.ds(0, MAIN)], w1_own, load_sem.at[0]),
        pltpu.make_async_copy(outer_ref.at[pl.ds(0, MAIN)], w2_own.at[pl.ds(128, MAIN)], load_sem.at[1]),
        pltpu.make_async_copy(tail_ref, w2_own.at[pl.ds(0, 128)], load_sem.at[2]),
    ]
    mine = pltpu.make_async_copy(patch_ref.at[pl.ds(pl.multiple_of(ROWS * mp, ROWS), ROWS)], xin.at[mp], own_sem)
    mine.start()
    loads[2].start()
    loads[0].start()
    loads[1].start()
    pl.semaphore_wait(barrier, len(peers))

    def patch_copy(rb, k):
        who = (mp + k) % 4
        return pltpu.make_async_remote_copy(
            src_ref=patch_ref.at[pl.ds(pl.multiple_of(ROWS * who + 128 * rb, 128), 128)],
            dst_ref=xin.at[mp, pl.ds(pl.multiple_of(128 * rb, 128), 128)],
            send_sem=patch_send.at[rb, k - 1], recv_sem=patch_recv.at[rb, k - 1],
            device_id=(dp, who), device_id_type=MESH)

    def start_patches(rb):
        for k in range(1, 4):
            patch_copy(rb, k).start()

    def piece(stage, kind, base=None, rows=None):
        if base is None:
            base, rows = stage_rows(stage)
        return pl.ds(pl.multiple_of(base + (kind * 4 + colour[kind]) * rows, 16), rows)

    def y_copy(stage, kind):
        rows = piece(stage, kind)
        src, dst = (w1_own, w1_oth) if stage < 5 else (w2_own, w2_oth)
        return pltpu.make_async_remote_copy(
            src_ref=src.at[rows], dst_ref=dst.at[rows],
            send_sem=y_send.at[stage, kind], recv_sem=y_recv.at[stage, kind],
            device_id=peers[LINK[stage, kind]], device_id_type=MESH)

    def side_copy(stage, kind, j, dst, base=None, rows=None):
        turn = 1 - 2 * (stage % 2)
        strong = ("xp", "xm") if kind == 0 else ("zp", "zm")
        if j < 2:
            who = peers[strong[j]]
        elif kind == 0:
            who = (dp_of(x, (z + turn + 8) % 8, yh), mp)
        else:
            who = (dp_of((x + turn + 4) % 4, z, yh), mp)
        rows = piece(stage, kind, base, rows)
        return pltpu.make_async_remote_copy(
            src_ref=dst.at[rows], dst_ref=dst.at[rows],
            send_sem=side_send.at[stage, kind, j], recv_sem=side_recv.at[stage, kind, j],
            device_id=who, device_id_type=MESH)

    def forward(stage, dst, base, rows):
        for kind in range(2):
            at = piece(stage, kind, base, rows)
            pltpu.make_async_remote_copy(
                src_ref=dst.at[at], dst_ref=dst.at[at], send_sem=y_send.at[stage, kind],
                recv_sem=y_recv.at[stage, kind], device_id=peers["hi"], device_id_type=MESH).wait_recv()
            for j in range(3):
                side_copy(stage, kind, j, dst, base, rows).start()

    def arrive(stage, dst, base, rows):
        for kind in range(2):
            for j in range(3):
                side_copy(stage, kind, j, dst, base, rows).wait_recv()

    start_patches(0)
    loads[2].wait()
    loads[0].wait()
    for stage in range(5):
        for kind in range(2):
            y_copy(stage, kind).start()
        if stage < 3:
            start_patches(stage + 1)
    loads[1].wait()
    for stage in range(5, 10):
        for kind in range(2):
            y_copy(stage, kind).start()
    forward(0, w1_oth, 0, 16)
    mine.wait()

    def norm_copy(rb):
        return pltpu.make_async_remote_copy(
            src_ref=xn.at[rb, core], dst_ref=xn.at[rb, core],
            send_sem=norm_send.at[rb], recv_sem=norm_recv.at[rb],
            device_id=peers["core"], device_id_type=MESH)

    def normalise(rb):
        for k in range(1, 4):
            patch_copy(rb, k).wait_recv()
        rows = pl.ds(pl.multiple_of(128 * rb, 128), 128)
        parts = [xin[m, rows, :] for m in range(4)]
        wide = [part.astype(F32) for part in parts]
        centre = sum(jnp.sum(part, axis=1, keepdims=True) for part in wide) * (1.0 / D)
        wide = [part - centre for part in wide]
        spread = sum(jnp.sum(part * part, axis=1, keepdims=True) for part in wide) * (1.0 / D)
        scale = lax.rsqrt(spread + epsilon)
        for m in range(4):
            xres[rows, DL * m:DL * m + DL] = parts[m]
            xn[rb, core, :, DL * m:DL * m + DL] = (wide[m] * scale).astype(BF16)
        norm_copy(rb).start()

    def own(rb):
        norm_copy(rb).wait_recv()
        block = xn[rb].reshape(256, D)
        for j in range(4):
            hid[:, 256 * j:256 * j + 256] = gelu(
                jnp.dot(block, w1_own[:, 256 * j:256 * j + 256], preferred_element_type=F32)).astype(BF16)
        acc[rb] = jnp.dot(hid[...], w2_own[128:, :], preferred_element_type=F32).reshape(2, 128, D)

    def first(rb, _):
        forward(rb + 1, w1_oth, pl.multiple_of(128 + 256 * rb, 128), 32)
        normalise(rb)

        @pl.when(rb > 0)
        def _():
            own(rb - 1)
        return 0
    lax.fori_loop(0, 4, first, 0)
    forward(5, w2_oth, 0, 16)
    own(3)
    arrive(0, w1_oth, 0, 16)
    def wait_inner(s, _):
        arrive(s + 1, w1_oth, pl.multiple_of(128 + 256 * s, 128), 32)
        return 0
    lax.fori_loop(0, 4, wait_inner, 0)

    def second(rb, _):
        block = xn[rb].reshape(256, D)
        for j in range(4):
            hid_oth[rb, :, 256 * j:256 * j + 256] = gelu(
                jnp.dot(block, w1_oth[:, 256 * j:256 * j + 256], preferred_element_type=F32)).astype(BF16)
        forward(rb + 6, w2_oth, pl.multiple_of(128 + 256 * rb, 128), 32)
        return 0
    lax.fori_loop(0, 4, second, 0)

    arrive(5, w2_oth, 0, 16)
    tail_in = jnp.concatenate([w2_own[0:TAIL, :], w2_oth[0:TAIL, :]], axis=0)
    tail_out = jnp.concatenate([w2_own[TAIL:2 * TAIL, :], w2_oth[TAIL:2 * TAIL, :]], axis=0)

    def tails(rb, _):
        block = xn[rb].reshape(256, D)
        units = gelu(lax.dot_general(block, tail_in, (((1,), (1,)), ((), ())), preferred_element_type=F32)).astype(BF16)
        acc[rb] += jnp.dot(units, tail_out, preferred_element_type=F32).reshape(2, 128, D)
        return 0
    lax.fori_loop(0, 4, tails, 0)

    for s in range(4):
        arrive(s + 6, w2_oth, 128 + 256 * s, 32)

        def mix(rb, _):
            acc[rb] += jnp.dot(
                hid_oth[rb, :, 256 * s:256 * s + 256], w2_oth[128 + 256 * s:384 + 256 * s, :],
                preferred_element_type=F32).reshape(2, 128, D)
            if s == 3:
                part_out[rb] = acc[rb, 1 - core].astype(BF16)
                part_copy(rb).start()
            return 0

        def part_copy(rb):
            return pltpu.make_async_remote_copy(
                src_ref=part_out.at[rb], dst_ref=part_in.at[rb], send_sem=part_send.at[rb],
                recv_sem=part_recv.at[rb], device_id=peers["core"], device_id_type=MESH)
        lax.fori_loop(0, 4, mix, 0)

    n0 = counts_ref[0]
    n1 = n0 + counts_ref[1]

    def finish(rb, sums):
        part_copy(rb).wait_recv()
        rows = pl.ds(pl.multiple_of(128 * rb, 128), 128)
        value = xres[rows, :].astype(F32) + (acc[rb, core] + part_in[rb].astype(F32))
        shifted = value - jnp.sum(value, axis=1, keepdims=True) * (1.0 / D)
        spread = jnp.sum(shifted * shifted, axis=1, keepdims=True) * (1.0 / D)
        scale = lax.rsqrt(spread + epsilon)
        ids = ROWS * mp + 128 * rb + lax.broadcasted_iota(jnp.int32, (128, 1), 0)
        normed = shifted * scale
        a = jnp.sum(jnp.where(ids < n0, normed, 0.0), axis=0, keepdims=True)
        b = jnp.sum(jnp.where((ids >= n0) & (ids < n1), normed, 0.0), axis=0, keepdims=True)
        return sums[0] + a, sums[1] + b
    zero = jnp.zeros((1, D), F32)
    a, b = lax.fori_loop(0, 4, finish, (zero, zero))
    out_ref[0:1, :] = a
    out_ref[1:2, :] = b

    def drain(rb, _):
        for k in range(1, 4):
            patch_copy(rb, k).wait_send()
        norm_copy(rb).wait_send()
        part_copy(rb).wait_send()
        return 0
    lax.fori_loop(0, 4, drain, 0)
    for stage in range(10):
        dst = w1_oth if stage < 5 else w2_oth
        for kind in range(2):
            y_copy(stage, kind).wait_send()
            for j in range(3):
                side_copy(stage, kind, j, dst).wait_send()


def main_scratch():
    dma = pltpu.SemaphoreType.DMA
    return [
        pltpu.VMEM((D, MAIN), BF16), pltpu.VMEM((D, D), BF16),
        pltpu.VMEM((D, MAIN), BF16), pltpu.VMEM((D, D), BF16),
        pltpu.VMEM((4, ROWS, DL), BF16), pltpu.VMEM((ROWS, D), BF16),
        pltpu.VMEM((4, 2, 128, D), BF16), pltpu.VMEM((4, 2, 128, D), F32),
        pltpu.VMEM((256, MAIN), BF16), pltpu.VMEM((4, 256, MAIN), BF16),
        pltpu.VMEM((4, 128, D), BF16), pltpu.VMEM((4, 128, D), BF16),
        dma((3,)), dma, dma((4, 3)), dma((4, 3)), dma((4,)), dma((4,)), dma((10, 2)), dma((10, 2)),
        dma((10, 2, 3)), dma((10, 2, 3)), dma((4,)), dma((4,)),
    ]


def image_sums(patches, inner, outer, counts):
    blank = jnp.zeros((TAIL - (inner.shape[1] - MAIN), D), BF16)
    tails = jnp.concatenate([inner[:, MAIN:].T, blank, outer[MAIN:], blank], axis=0)
    vmem, smem = pl.BlockSpec(memory_space=pltpu.VMEM), pl.BlockSpec(memory_space=pltpu.SMEM)
    hbm = pl.BlockSpec(memory_space=pl.ANY)
    return pl.pallas_call(
        main_kernel,
        out_shape=jax.ShapeDtypeStruct((2, D), F32),
        in_specs=[hbm, hbm, hbm, hbm, smem],
        out_specs=vmem,
        scratch_shapes=main_scratch(),
        compiler_params=pltpu.CompilerParams(
            collective_id=2, has_side_effects=True, vmem_limit_bytes=56 * 2**20),
        name="tower",
    )(patches, inner, outer, tails, counts)


def shards(
    patches, counts, pair_ids, inner_weight, outer_weight, text_embed, log_scale, logit_bias
):
    sums = image_sums(patches, inner_weight, outer_weight, counts)
    return tail(sums, text_embed, counts, pair_ids, log_scale, logit_bias)


def solution(mesh):
    placed = (
        P("dp", "mp"),
        P("dp"),
        P("dp"),
        P(None, "mp"),
        P("mp", None),
        P("dp", "mp"),
        P(),
        P(),
    )
    return jax.shard_map(
        shards,
        mesh=mesh,
        in_specs=placed,
        out_specs=(P("dp"), P("dp", "mp"), P("dp", "mp")),
        check_vma=False,
    )
```

```python
import functools

import jax
import jax.numpy as jnp
from jax import lax
from jax.experimental import pallas as pl
from jax.experimental.pallas import tpu as pltpu
from jax.sharding import PartitionSpec as P

MESH = pl.DeviceIdType.MESH
epsilon = 1e-06
D = 1152
DL = 288
F32, BF16 = jnp.float32, jnp.bfloat16


def coords():
    dp, mp = lax.axis_index("dp"), lax.axis_index("mp")
    return dp // 16, (dp // 2) % 8, dp % 2, mp


def dp_of(x, z, yh):
    return x * 16 + z * 2 + yh


def tail_peers():
    x, z, yh, mp = coords()
    dp = dp_of(x, z, yh)
    group = [(dp, (mp + k) % 4) for k in range(1, 4)]
    line = [(dp_of(x, (z + k) % 8, yh), mp) for k in range(1, 8)]
    plane = [(dp_of((x + k // 2) % 4, z, (yh + k) % 2), mp) for k in range(1, 8)]
    return group, line, plane


def tail_body(
    counts_ref, pair_ref, scale_ref, bias_ref, loss_ref, emb_ref, txt_ref,
    sums, rows, packed, msg, dots, group_send, group_recv, line_send, line_recv,
    plane_send, plane_recv, dots_send, dots_recv, meanwhile,
):
    x, z, yh, mp = coords()
    group, line, plane = tail_peers()
    dp = dp_of(x, z, yh)
    slot = (x * 2 + yh) * 8 + z

    copies = []
    for k, peer in enumerate(group):
        copies.append(pltpu.make_async_remote_copy(
            src_ref=sums.at[mp], dst_ref=sums.at[mp], send_sem=group_send.at[k],
            recv_sem=group_recv.at[k], device_id=peer, device_id_type=MESH))
        copies[-1].start()
    meanwhile()
    for copy in copies:
        copy.wait_recv()
    total = ((sums[0] + sums[1]) + sums[2]) + sums[3]
    row = lax.broadcasted_iota(jnp.int32, (8, 1), 0)
    count = jnp.where(row == 0, counts_ref[0], jnp.where(row == 1, counts_ref[1], 1)).astype(F32)
    values = total / count
    norm = lax.rsqrt(jnp.sum(values * values, axis=1, keepdims=True) + epsilon)
    unit = values * norm
    rows[:, :D] = unit
    rows[:, D:] = jnp.zeros((8, rows.shape[1] - D), F32)
    lane = lax.broadcasted_iota(jnp.int32, (4, 128), 1)
    units = []
    for b in range(3):
        block = jnp.zeros((4, 128), F32)
        for k in range(4):
            block = jnp.where(mp == k, rows[0:4, DL * k + 128 * b: DL * k + 128 * b + 128], block)
        if b == 2:
            block = jnp.where(lane < DL - 256, block, 0.0)
        units.append(block)
        packed[4 * b:4 * b + 4, :] = block
    line4 = lax.broadcasted_iota(jnp.int32, (4, 128), 0)
    packed[12:16, :] = jnp.where(
        line4 == 0, pair_ref[0].astype(F32), jnp.where(line4 == 1, pair_ref[1].astype(F32), 0.0))
    msg[slot] = packed[...].astype(BF16)

    sends = []
    for k, peer in enumerate(line):
        sends.append(pltpu.make_async_remote_copy(
            src_ref=msg.at[slot], dst_ref=msg.at[slot], send_sem=line_send.at[k],
            recv_sem=line_recv.at[k], device_id=peer, device_id_type=MESH))
        sends[-1].start()
    row16 = lax.broadcasted_iota(jnp.int32, (16, 128), 0)
    lane16 = lax.broadcasted_iota(jnp.int32, (16, 128), 1)
    for b in range(3):
        wire = units[b].astype(BF16).astype(F32)
        packed[0:4, :] = wire
        packed[4:8, :] = units[b] - wire
        packed[8:16, :] = jnp.zeros((8, 128), F32)
        left = packed[...]
        if b == 0:
            left = jnp.where((row16 == 8) & (lane16 == 0), 1.0, left)
        rows_b = left.astype(BF16)
        lefts = [rows_b] if b == 0 else lefts + [rows_b]
    left = jnp.concatenate(lefts, axis=0)
    for copy in sends:
        copy.wait_recv()
    first = (x * 2 + yh) * 8
    for k, peer in enumerate(plane):
        sends.append(pltpu.make_async_remote_copy(
            src_ref=msg.at[pl.ds(first, 8)], dst_ref=msg.at[pl.ds(first, 8)], send_sem=plane_send.at[k],
            recv_sem=plane_recv.at[k], device_id=peer, device_id_type=MESH))
        sends[-1].start()
    for copy in sends[7:]:
        copy.wait_recv()
    everyone = msg[...].reshape(1024, 128)
    prod = lax.dot_general(left, everyone, (((1,), (1,)), ((), ())), preferred_element_type=F32)
    pairs = pltpu.roll(prod[0:16], 1024 - 12, 1)[8:9]
    part = prod[0:16] + pltpu.roll(prod[16:32], 1024 - 4, 1) + pltpu.roll(prod[32:48], 1024 - 8, 1)
    dots[mp] = part[0:8]
    swaps = []
    for k, peer in enumerate(group):
        swaps.append(pltpu.make_async_remote_copy(
            src_ref=dots.at[mp], dst_ref=dots.at[mp], send_sem=dots_send.at[k],
            recv_sem=dots_recv.at[k], device_id=peer, device_id_type=MESH))
        swaps[-1].start()
    for copy in swaps:
        copy.wait_recv()
    dot = ((dots[0] + dots[1]) + dots[2]) + dots[3]
    column = lax.broadcasted_iota(jnp.int32, (8, 1024), 1)
    place, kind = column // 16, column % 16
    shard = (place // 16) * 16 + (place % 8) * 2 + (place // 8) % 2
    row8 = lax.broadcasted_iota(jnp.int32, (8, 1024), 0)
    own_pair = jnp.where(row8 == 0, pair_ref[0], pair_ref[1])
    all_pair = jnp.broadcast_to(pairs, (8, 1024)).astype(jnp.int32)
    wanted = jnp.where(row8 < 2, own_pair, all_pair)
    match = wanted == jnp.where(row8 < 2, shard * 2 + kind - 2, dp * 2 + row8 - 2)
    valid = ((row8 < 2) & ((kind == 2) | (kind == 3))) | ((row8 >= 2) & (row8 < 4) & (kind < 2))
    scale = jnp.exp(jnp.full((8, 1024), scale_ref[0], F32))
    label = jnp.where(match, 1.0, -1.0)
    turned = -label * (scale * dot + bias_ref[0])
    small = jnp.exp(-jnp.abs(turned))
    soft = jnp.where(valid, jnp.maximum(turned, 0.0) + jnp.log1p(small), 0.0)
    sigmoid = jnp.where(turned >= 0, 1.0, small) / (1.0 + small)
    slope = jnp.where(valid, -label * sigmoid, 0.0)
    loss = jnp.sum(soft, axis=1, keepdims=True)
    whole = dot + pltpu.roll(dot, 4, 0)
    proj = jnp.sum(scale * slope * whole, axis=1, keepdims=True)[0:4]
    high = slope.astype(BF16)
    rest = slope - high.astype(F32)
    mid = rest.astype(BF16)
    low = (rest - mid.astype(F32)).astype(BF16)
    stack = jnp.concatenate([high.astype(F32), mid.astype(F32), low.astype(F32)], axis=0)
    stack = jnp.concatenate([stack, pltpu.roll(stack, 4, 1), pltpu.roll(stack, 8, 1)], axis=0).astype(BF16)
    dirs = jnp.dot(stack, everyone, preferred_element_type=F32)
    for b in range(3):
        own = dirs[24 * b:24 * b + 24]
        direction = (own[0:8] + (own[8:16] + own[16:24]))[0:4] * scale[0:4, 0:128]
        grad = (direction - units[b] * proj) * norm[0:4]
        width = 128 if b < 2 else DL - 256
        emb_ref[:, 128 * b:128 * b + width] = grad[0:2, :width]
        txt_ref[:, 128 * b:128 * b + width] = grad[2:4, :width]
    loss_ref[...] = jnp.broadcast_to(loss[0:2], (2, 128))
    for copy in copies + sends + swaps:
        copy.wait_send()


def tail_scratch():
    dma = pltpu.SemaphoreType.DMA
    return [
        pltpu.VMEM((4, 8, D), F32),
        pltpu.VMEM((8, D + 128), F32),
        pltpu.VMEM((16, 128), F32),
        pltpu.VMEM((64, 16, 128), BF16),
        pltpu.VMEM((4, 8, 1024), F32),
        dma((3,)), dma((3,)), dma((7,)), dma((7,)), dma((7,)), dma((7,)), dma((3,)), dma((3,)),
    ]


ROWS = 512
MAIN = 1024
TAIL = 64
WINDOW = 2
STAGES = 9
LINK = {}
for _s in range(STAGES):
    for _k in range(2):
        LINK[_s, _k] = "hi" if _s < 5 else ("hi", "lo")[_k]


def main_peers():
    x, z, yh, mp = coords()
    dp = dp_of(x, z, yh)
    return dict(
        core=(dp, mp + 1 - 2 * (mp % 2)),
        lo=(dp, (mp + 2) % 4),
        cross=(dp, 3 - mp),
        hi=(dp + 1 - 2 * (dp % 2), (mp + 2) % 4),
        xp=(dp_of((x + 1) % 4, z, yh), mp),
        xm=(dp_of((x + 3) % 4, z, yh), mp),
        zp=(dp_of(x, (z + 1) % 8, yh), mp),
        zm=(dp_of(x, (z + 7) % 8, yh), mp),
    )


def gelu(u):
    inner = u * (0.7978845608028654 + 0.035677408136300125 * (u * u))
    half = 0.5 * u
    return half + half * jnp.tanh(inner)


def main_kernel(
    patch_ref, inner_ref, outer_ref, inner_tail, outer_tail, text_ref, counts_ref, pair_ref, scale_ref, bias_ref,
    loss_ref, emb_ref, txt_ref,
    w1_own, w2_own, w1_oth, w2_oth, xin, xres, xn, acc, hid, part_out, part_in,
    load_sem, own_sem, patch_send, patch_recv, norm_send, norm_recv, y_send, y_recv,
    side_send, side_recv, part_send, part_recv, *tail_refs,
):
    x, z, yh, mp = coords()
    dp = dp_of(x, z, yh)
    core = mp % 2
    colour = [(x + 2 * z) % 4, (2 * x + z) % 4]
    peers = main_peers()
    barrier = pltpu.get_barrier_semaphore()
    group, line, plane = tail_peers()
    everyone = [peers["hi"]] + group + line + plane
    for peer in everyone:
        pl.semaphore_signal(barrier, inc=1, device_id=peer, device_id_type=MESH)
    mains = pl.ds(2 * TAIL, MAIN)
    loads = [
        pltpu.make_async_copy(inner_ref.at[pl.ds(0, MAIN)], w1_own.at[mains], load_sem.at[0]),
        pltpu.make_async_copy(outer_ref.at[pl.ds(0, MAIN)], w2_own.at[mains], load_sem.at[1]),
    ]
    mine = [
        pltpu.make_async_copy(
            patch_ref.at[:, pl.ds(pl.multiple_of(ROWS * mp + 128 * rb, 128), 128)], xin.at[rb, mp], own_sem.at[rb])
        for rb in range(4)]
    for copy in loads + mine:
        copy.start()
    live = lax.broadcasted_iota(jnp.int32, (TAIL, 1), 0) < inner_ref.shape[0] - MAIN
    for tail_ref, own, oth in ((inner_tail, w1_own, w1_oth), (outer_tail, w2_own, w2_oth)):
        value = jnp.where(live, tail_ref[...].astype(F32), 0.0).astype(BF16)
        own[0:TAIL, :] = value
        oth[TAIL:2 * TAIL, :] = value
    sums = tail_refs[0]
    sums[mp] = jnp.zeros((8, D), F32)
    for k in range(4):
        @pl.when(mp == k)
        def _():
            sums[k, 2:4, DL * k:DL * k + DL] = text_ref[...].astype(F32)
    pl.semaphore_wait(barrier, len(everyone))

    def patch_copy(rb, k):
        who = (mp + k) % 4
        return pltpu.make_async_remote_copy(
            src_ref=patch_ref.at[:, pl.ds(pl.multiple_of(ROWS * who + 128 * rb, 128), 128)],
            dst_ref=xin.at[rb, mp],
            send_sem=patch_send.at[rb, k - 1], recv_sem=patch_recv.at[rb, k - 1],
            device_id=(dp, who), device_id_type=MESH)

    def start_patches(rb):
        for k in range(1, 4):
            patch_copy(rb, k).start()

    def places(stage):
        if stage == 0:
            return [(k, (w1_own, w2_own)[k], (w1_oth, w2_oth)[k],
                     pl.ds(pl.multiple_of(colour[k] * 16, 16), 16)) for k in range(2)]
        own, oth = (w1_own, w1_oth) if stage < 5 else (w2_own, w2_oth)
        base = 128 + 256 * ((stage - 1) % 4)
        return [(k, own, oth, pl.ds(pl.multiple_of(base + 128 * k + colour[k] * 32, 32), 32)) for k in range(2)]

    def y_copies(stage):
        return [pltpu.make_async_remote_copy(
            src_ref=own.at[rows], dst_ref=oth.at[rows],
            send_sem=y_send.at[stage, k], recv_sem=y_recv.at[stage, k],
            device_id=peers[LINK[stage, k]], device_id_type=MESH) for k, own, oth, rows in places(stage)]

    def side_copies(stage):
        copies = []
        for k, own, oth, rows in places(stage):
            near = ("xp", "xm") if k == 0 else ("zp", "zm")
            far = ("zp", "zm") if k == 0 else ("xp", "xm")
            for j, who in enumerate((near[0], near[1], far[stage % 2])):
                copies.append(pltpu.make_async_remote_copy(
                    src_ref=oth.at[rows], dst_ref=oth.at[rows],
                    send_sem=side_send.at[stage, k, j], recv_sem=side_recv.at[stage, k, j],
                    device_id=peers[who], device_id_type=MESH))
        return copies

    def send_y(stage):
        if stage < STAGES:
            for copy in y_copies(stage):
                copy.start()

    def forward(stage):
        side = side_copies(stage)
        for k, copy in enumerate(y_copies(stage)):
            copy.wait_recv()
            for j in range(3):
                side[3 * k + j].start()
        for copy in y_copies(stage):
            copy.wait_send()
        send_y(stage + WINDOW)

    def arrive(stage):
        for copy in side_copies(stage):
            copy.wait_recv()

    def norm_copy(rb):
        at = (rb // 2, (rb % 2) * 2 + core)
        return pltpu.make_async_remote_copy(
            src_ref=xn.at[at], dst_ref=xn.at[at], send_sem=norm_send.at[rb], recv_sem=norm_recv.at[rb],
            device_id=peers["core"], device_id_type=MESH)

    def normalise(rb):
        mine[rb].wait()
        for k in range(1, 4):
            patch_copy(rb, k).wait_recv()
        if rb + 2 < 4:
            start_patches(rb + 2)
        raw = xin[rb].reshape(D, 128)
        wide = raw.astype(F32)
        wide = wide - jnp.sum(wide, axis=0, keepdims=True) * (1.0 / D)
        spread = jnp.sum(wide * wide, axis=0, keepdims=True) * (1.0 / D)
        xn[rb // 2, (rb % 2) * 2 + core] = (wide * lax.rsqrt(spread + epsilon)).astype(BF16).T
        norm_copy(rb).start()
        xres[rb] = raw.T

    def expand(half, weights, first, count):
        block = xn[half].reshape(512, D)
        for j in range(count):
            lo = first + 256 * j if first or j else 0
            hi = first + 256 * (j + 1)
            hid[half, :, lo:hi] = gelu(lax.dot_general(
                block, weights[lo:hi, :], (((1,), (1,)), ((), ())), preferred_element_type=F32)).astype(BF16)

    def mix(half, weights, lo, hi, fresh):
        term = jnp.dot(hid[half, :, lo:hi], weights[lo:hi, :], preferred_element_type=F32).reshape(4, 128, D)
        acc[half] = term if fresh else acc[half] + term

    def part_copy(rb):
        return pltpu.make_async_remote_copy(
            src_ref=part_out.at[rb], dst_ref=part_in.at[rb], send_sem=part_send.at[rb],
            recv_sem=part_recv.at[rb], device_id=peers["core"], device_id_type=MESH)

    start_patches(0)
    loads[0].wait()
    for s in range(WINDOW):
        send_y(s)
    start_patches(1)
    forward(0)
    normalise(0)
    forward(1)
    normalise(1)
    forward(2)
    loads[1].wait()
    for half in range(2):
        norm_copy(2 * half).wait_recv()
        norm_copy(2 * half + 1).wait_recv()
        expand(half, w1_own, 128, 4)
        forward(3 + 2 * half)
        mix(half, w2_own, 128, 1152, True)
        if half == 0:
            normalise(2)
            forward(4)
            normalise(3)
    for s in range(5):
        arrive(s)

    def hidden(half, _):
        block = xn[half].reshape(512, D)
        for lo, hi in ((0, 128), (128, 384), (384, 640), (640, 896), (896, 1152)):
            hid[half, :, lo:hi] = gelu(lax.dot_general(
                block, w1_oth[lo:hi, :], (((1,), (1,)), ((), ())), preferred_element_type=F32)).astype(BF16)
        return 0
    hidden(0, 0)
    forward(6)
    hidden(1, 0)
    forward(7)
    forward(8)
    arrive(5)
    arrive(6)
    mix(0, w2_oth, 0, 640, False)
    mix(1, w2_oth, 0, 640, False)
    arrive(7)
    arrive(8)
    for half in range(2):
        mix(half, w2_oth, 640, 1152, False)
        for r in range(2):
            rb = half * 2 + r
            part_out[rb] = acc[half, 2 * r + 1 - core].astype(BF16)
            part_copy(rb).start()

    n0 = counts_ref[0]
    n1 = n0 + counts_ref[1]

    def finish(rb, sums):
        part_copy(rb).wait_recv()
        value = xres[rb].astype(F32) + (acc[rb // 2, (rb % 2) * 2 + core] + part_in[rb].astype(F32))
        shifted = value - jnp.sum(value, axis=1, keepdims=True) * (1.0 / D)
        spread = jnp.sum(shifted * shifted, axis=1, keepdims=True) * (1.0 / D)
        scale = lax.rsqrt(spread + epsilon)
        ids = ROWS * mp + 128 * rb + lax.broadcasted_iota(jnp.int32, (128, 1), 0)
        normed = shifted * scale
        a = jnp.sum(jnp.where(ids < n0, normed, 0.0), axis=0, keepdims=True)
        b = jnp.sum(jnp.where((ids >= n0) & (ids < n1), normed, 0.0), axis=0, keepdims=True)
        return sums[0] + a, sums[1] + b
    zero = jnp.zeros((1, D), F32)
    a, b = lax.fori_loop(0, 4, finish, (zero, zero))
    sums[mp, 0:1, :] = a
    sums[mp, 1:2, :] = b

    def drain():
        for rb in range(4):
            for k in range(1, 4):
                patch_copy(rb, k).wait_send()
            norm_copy(rb).wait_send()
            part_copy(rb).wait_send()
        for stage in range(STAGES):
            for copy in side_copies(stage):
                copy.wait_send()
    tail_body(counts_ref, pair_ref, scale_ref, bias_ref, loss_ref, emb_ref, txt_ref, *tail_refs, drain)


def main_scratch():
    dma = pltpu.SemaphoreType.DMA
    return [
        pltpu.VMEM((D, D), BF16), pltpu.VMEM((D, D), BF16), pltpu.VMEM((D, D), BF16), pltpu.VMEM((D, D), BF16),
        pltpu.VMEM((4, 4, DL, 128), BF16), pltpu.VMEM((4, 128, D), BF16),
        pltpu.VMEM((2, 4, 128, D), BF16), pltpu.VMEM((2, 4, 128, D), F32),
        pltpu.VMEM((2, 512, D), BF16),
        pltpu.VMEM((4, 128, D), BF16), pltpu.VMEM((4, 128, D), BF16),
        dma((2,)), dma((4,)), dma((4, 3)), dma((4, 3)), dma((4,)), dma((4,)), dma((STAGES, 2)), dma((STAGES, 2)),
        dma((STAGES, 2, 3)), dma((STAGES, 2, 3)), dma((4,)), dma((4,)),
    ]


def hand_over(loss_ref, emb_ref, txt_ref, loss_out, emb_out, txt_out):
    emb_out[...] = emb_ref[...]
    txt_out[...] = txt_ref[...]
    loss_out[0] = loss_ref[0, 0]
    loss_out[1] = loss_ref[1, 0]


def shards(
    patches, counts, pair_ids, inner_weight, outer_weight, text_embed, log_scale, logit_bias
):
    vmem, smem = pl.BlockSpec(memory_space=pltpu.VMEM), pl.BlockSpec(memory_space=pltpu.SMEM)
    hbm = pl.BlockSpec(memory_space=pl.ANY)
    end = pl.BlockSpec((TAIL, D), lambda i: (MAIN // TAIL, 0))
    half = jax.ShapeDtypeStruct((2, DL), F32)
    inner = inner_weight.T
    found = pl.pallas_call(
        main_kernel,
        grid=(1,),
        out_shape=(jax.ShapeDtypeStruct((2, 128), F32), half, half),
        in_specs=[hbm, hbm, hbm, end, end, vmem, smem, smem, smem, smem],
        out_specs=(vmem, vmem, vmem),
        scratch_shapes=main_scratch() + tail_scratch(),
        compiler_params=pltpu.CompilerParams(
            collective_id=1, has_side_effects=True, vmem_limit_bytes=56 * 2**20),
        name="tower",
    )(patches.T, inner, outer_weight, inner, outer_weight, text_embed, counts, pair_ids, log_scale, logit_bias)
    return pl.pallas_call(
        hand_over,
        out_shape=(jax.ShapeDtypeStruct((2,), F32), half, half),
        in_specs=[vmem, vmem, vmem],
        out_specs=(smem, vmem, vmem),
        name="hand_over",
    )(*found)


def solution(mesh):
    placed = (
        P("dp", "mp"),
        P("dp"),
        P("dp"),
        P(None, "mp"),
        P("mp", None),
        P("dp", "mp"),
        P(),
        P(),
    )
    return jax.shard_map(
        shards,
        mesh=mesh,
        in_specs=placed,
        out_specs=(P("dp"), P("dp", "mp"), P("dp", "mp")),
        check_vma=False,
    )
```

```python
import functools

import jax
import jax.numpy as jnp
from jax import lax
from jax.experimental import pallas as pl
from jax.experimental.pallas import tpu as pltpu
from jax.sharding import PartitionSpec as P

MESH = pl.DeviceIdType.MESH
epsilon = 1e-06
D = 1152
DL = 288
F32, BF16 = jnp.float32, jnp.bfloat16


def coords():
    dp, mp = lax.axis_index("dp"), lax.axis_index("mp")
    return dp // 16, (dp // 2) % 8, dp % 2, mp


def dp_of(x, z, yh):
    return x * 16 + z * 2 + yh


def tail_peers():
    x, z, yh, mp = coords()
    dp = dp_of(x, z, yh)
    group = [(dp, (mp + k) % 4) for k in range(1, 4)]
    line = [(dp_of(x, (z + k) % 8, yh), mp) for k in range(1, 8)]
    plane = [(dp_of((x + k // 2) % 4, z, (yh + k) % 2), mp) for k in range(1, 8)]
    return group, line, plane


def by_parity(column, even, odd):
    return jnp.where(column % 2 == 0, even, odd)


def parity_sums(values):
    own = jnp.sum(values, axis=1, keepdims=True)
    row = lax.broadcasted_iota(jnp.int32, own.shape, 0)
    even = jnp.sum(jnp.where(row % 2 == 0, own, 0.0), axis=0, keepdims=True)
    odd = jnp.sum(jnp.where(row % 2 == 1, own, 0.0), axis=0, keepdims=True)
    return even, odd


def three_terms(values):
    high = values.astype(BF16).astype(F32)
    rest = values - high
    mid = rest.astype(BF16).astype(F32)
    return jnp.concatenate([high, mid, rest - mid], axis=0).astype(BF16)


def stacked(wide):
    return jnp.concatenate([wide[:, 128 * q:128 * q + 128] for q in range(4)], axis=0)


def folded(dots):
    return dots[0:2] + pltpu.roll(dots, 512 - 2, 1)[2:4] + pltpu.roll(dots, 512 - 4, 1)[4:6]


class Tail:
    def __init__(self, text_ref, counts_ref, pair_ref, scale_ref, bias_ref, loss_ref, emb_ref, txt_ref,
                 psum, tss, wide, units, tline, iline, tall, iall, pairs, dots, *sems):
        self.__dict__.update(locals())
        self.x, self.z, self.yh, self.mp = coords()
        self.dp = dp_of(self.x, self.z, self.yh)
        self.own_line = self.x * 2 + self.yh
        self.group, self.line, self.plane = tail_peers()
        self.copies = {}

    def send(self, name, sem, ref, peers):
        sent, got = self.sems[2 * sem], self.sems[2 * sem + 1]
        self.copies[name] = [pltpu.make_async_remote_copy(
            src_ref=ref, dst_ref=ref, send_sem=sent.at[k], recv_sem=got.at[k],
            device_id=peer, device_id_type=MESH) for k, peer in enumerate(peers)]
        for copy in self.copies[name]:
            copy.start()

    def take(self, name):
        for copy in self.copies[name]:
            copy.wait_recv()

    def begin(self):
        text = self.text_ref[...].astype(F32)
        self.tss[self.mp] = jnp.zeros((8, 128), F32)
        self.tss[self.mp, 0:2, :] = jnp.broadcast_to(jnp.sum(text * text, axis=1, keepdims=True), (2, 128))
        self.units[...] = jnp.zeros((4, 8, 128), F32)
        for b in range(3):
            width = 128 if b < 2 else DL - 256
            self.units[0, 2 * b:2 * b + 2, 0:width] = text[:, 128 * b:128 * b + width]
        self.wide[...] = jnp.zeros((8, D + 128), F32)

    def greet(self):
        self.send("tss", 0, self.tss.at[self.mp], self.group)

    def text_line(self):
        self.take("tss")
        total = ((self.tss[0] + self.tss[1]) + self.tss[2]) + self.tss[3]
        norm = lax.rsqrt(total + epsilon)
        row = lax.broadcasted_iota(jnp.int32, (8, 128), 0)
        norm = by_parity(row, norm[0:1], norm[1:2])
        unit = self.units[0] * norm
        self.units[0] = unit
        self.units[1] = norm
        wire = unit.astype(BF16).astype(F32)
        ids = jnp.where(row == 6, self.pair_ref[0], self.pair_ref[1]).astype(F32)
        self.tline[self.z] = jnp.where(row < 6, wire, ids)
        self.send("tline", 1, self.tline.at[self.z], self.line)

    def text_plane(self):
        self.take("tline")
        self.tall[self.own_line] = self.tline[...].reshape(64, 128).astype(BF16)
        self.send("tplane", 2, self.tall.at[self.own_line], self.plane)

    def text_done(self):
        self.take("tplane")
        first = (lax.broadcasted_iota(jnp.int32, (16, 128), 1) == 0).astype(F32).astype(BF16)
        column = lax.dot_general(
            first, self.tall[...].reshape(512, 128), (((1,), (1,)), ((), ())), preferred_element_type=F32)
        self.pairs[...] = pltpu.roll(stacked(column[0:2]), 128 - 4, 1)

    def image_line(self, first, second):
        self.psum[self.mp, 0:1, :] = first
        self.psum[self.mp, 1:2, :] = second
        self.send("psum", 3, self.psum.at[self.mp], self.group)

    def image_rows(self):
        self.take("psum")
        psum, mp = self.psum, self.mp
        row = lax.broadcasted_iota(jnp.int32, (2, 1), 0)
        count = jnp.where(row == 0, self.counts_ref[0], self.counts_ref[1]).astype(F32)
        pooled = (((psum[0] + psum[1]) + psum[2]) + psum[3]) / count
        norm = lax.rsqrt(jnp.sum(pooled * pooled, axis=1, keepdims=True) + epsilon)
        self.wide[0:2, :D] = pooled * norm
        lane = lax.broadcasted_iota(jnp.int32, (2, 128), 1)
        for b in range(3):
            block = self.wide[0:2, 128 * b:128 * b + 128]
            for k in range(1, 4):
                block = jnp.where(mp == k, self.wide[0:2, DL * k + 128 * b:DL * k + 128 * b + 128], block)
            self.units[2, 2 * b:2 * b + 2, :] = block if b < 2 else jnp.where(lane < DL - 256, block, 0.0)
        row8 = lax.broadcasted_iota(jnp.int32, (8, 128), 0)
        unit = self.units[2]
        self.units[3] = by_parity(row8, norm[0:1], norm[1:2]) + jnp.zeros((8, 128), F32)
        wire = unit.astype(BF16).astype(F32)
        self.iline[self.z] = wire
        self.send("iline", 4, self.iline.at[self.z], self.line)

    def left(self, unit):
        wire = unit.astype(BF16).astype(F32)
        return jnp.concatenate([wire, unit - wire], axis=0).astype(BF16)

    def against(self, unit, everyone):
        found = lax.dot_general(
            self.left(unit), everyone, (((1,), (1,)), ((), ())), preferred_element_type=F32)
        return folded(found[0:8]), folded(found[8:16])

    def end(self, meanwhile):
        texts = self.tall[...].reshape(512, 128)
        image, image_rest = self.against(self.units[2], texts)
        self.take("iline")
        self.iall[self.own_line] = self.iline[...].reshape(64, 128).astype(BF16)
        self.send("iplane", 5, self.iall.at[self.own_line], self.plane)
        meanwhile()
        self.take("iplane")
        images = self.iall[...].reshape(512, 128)
        text, text_rest = self.against(self.units[0], images)
        kind = lax.broadcasted_iota(jnp.int32, (2, 512), 1) % 8
        mixed = jnp.where(kind < 2, image, jnp.where(
            kind < 4, pltpu.roll(text, 2, 1), jnp.where(
                kind < 6, pltpu.roll(image_rest, 4, 1), pltpu.roll(text_rest, 6, 1))))
        self.dots[self.mp] = stacked(mixed)
        self.send("dots", 6, self.dots.at[self.mp], self.group)
        row = lax.broadcasted_iota(jnp.int32, (8, 128), 0)
        lane = lax.broadcasted_iota(jnp.int32, (8, 128), 1)
        column = (row // 2) * 128 + lane
        kind = column % 8
        place = column // 64
        shard = (place // 2) * 16 + ((column // 8) % 8) * 2 + place % 2
        other = shard * 2 + kind % 2
        own = row % 2
        own_pair = by_parity(row, self.pair_ref[0], self.pair_ref[1])
        match = jnp.where(kind < 2, own_pair, self.pairs[...].astype(jnp.int32)) == jnp.where(
            kind < 2, other, self.dp * 2 + own)
        label = jnp.where(match, 1.0, -1.0)
        scale = jnp.exp(jnp.full((8, 128), self.scale_ref[0], F32))
        self.take("dots")
        dots = self.dots
        dot = ((dots[0] + dots[1]) + dots[2]) + dots[3]
        turned = -label * (scale * dot + self.bias_ref[0])
        small = jnp.exp(-jnp.abs(turned))
        soft = jnp.where(kind < 2, jnp.maximum(turned, 0.0) + jnp.log1p(small), 0.0)
        sigmoid = jnp.where(turned >= 0, 1.0, small) / (1.0 + small)
        slope = jnp.where(kind < 4, -label * sigmoid, 0.0)
        term = scale * slope * (dot + pltpu.roll(dot, 128 - 4, 1))
        loss = parity_sums(soft)
        image_proj = parity_sums(jnp.where(kind < 2, term, 0.0))
        text_proj = parity_sums(jnp.where(kind >= 2, term, 0.0))
        blank = jnp.zeros((2, 512), F32)
        for everyone, kept, proj, at, out in (
            (texts, kind < 2, image_proj, 2, self.emb_ref), (images, kind >= 2, text_proj, 0, self.txt_ref)
        ):
            flat = jnp.where(kept, slope, 0.0)
            flat = jnp.concatenate([flat[2 * q:2 * q + 2] for q in range(4)], axis=1)
            if at == 0:
                flat = pltpu.roll(flat, 512 - 2, 1)
            spread = jnp.concatenate([flat, pltpu.roll(flat, 2, 1), pltpu.roll(flat, 4, 1), blank], axis=0)
            found = jnp.dot(three_terms(spread), everyone, preferred_element_type=F32)
            direction = (found[0:8] + (found[8:16] + found[16:24])) * scale
            grad = (direction - self.units[at] * by_parity(row, proj[0], proj[1])) * self.units[at + 1]
            for b in range(3):
                width = 128 if b < 2 else DL - 256
                out[:, 128 * b:128 * b + width] = grad[2 * b:2 * b + 2, 0:width]
        self.loss_ref[...] = by_parity(lax.broadcasted_iota(jnp.int32, (2, 128), 0), loss[0], loss[1])
        for copies in self.copies.values():
            for copy in copies:
                copy.wait_send()


def tail_scratch():
    dma = pltpu.SemaphoreType.DMA
    pair = lambda n: [dma((n,)), dma((n,))]
    return [
        pltpu.VMEM((4, 2, D), F32), pltpu.VMEM((4, 8, 128), F32), pltpu.VMEM((8, D + 128), F32),
        pltpu.VMEM((4, 8, 128), F32), pltpu.VMEM((8, 8, 128), F32), pltpu.VMEM((8, 8, 128), F32),
        pltpu.VMEM((8, 64, 128), BF16), pltpu.VMEM((8, 64, 128), BF16), pltpu.VMEM((8, 128), F32),
        pltpu.VMEM((4, 8, 128), F32),
    ] + pair(3) + pair(7) + pair(7) + pair(3) + pair(7) + pair(7) + pair(3)


ROWS = 512
MAIN = 1024
TAIL = 64
WINDOW = 4
STAGES = 9
HI = [(0, 0), (0, 1), (1, 0), (1, 1), (2, 0), (2, 1), (3, 1), (4, 0), (5, 1), (6, 0), (6, 1), (7, 1)]
LO = [('P', 0), ('P', 1), (3, 0), ('P', 2), (4, 1), ('P', 3), (5, 0), (7, 0), (8, 0), (8, 1)]
ORDER = [('F', 0, 0), ('F', 0, 1), ('N', 0), ('F', 1, 0), ('F', 1, 1), ('N', 1), ('F', 2, 0), ('F', 3, 0), ('F', 2, 1), ('E', 0, 0), ('E', 0, 1), ('E', 0, 2), ('E', 0, 3), ('F', 3, 1), ('M', 0, 0), ('N', 2), ('F', 4, 0), ('M', 0, 1), ('F', 4, 1), ('H', 0, 0), ('F', 5, 1), ('H', 0, 1), ('H', 0, 2), ('H', 0, 3), ('F', 6, 0), ('N', 3), ('F', 6, 1), ('H', 0, 4), ('F', 5, 0), ('F', 7, 1), ('E', 1, 0), ('E', 1, 1), ('E', 1, 2), ('F', 7, 0), ('E', 1, 3), ('M', 1, 0), ('F', 8, 0), ('M', 1, 1), ('H', 1, 0), ('H', 1, 1), ('F', 8, 1), ('H', 1, 2), ('H', 1, 3), ('H', 1, 4), ('A', 0, 0), ('A', 0, 1), ('A', 1, 0), ('A', 1, 1), ('B', 0), ('B', 1)]


def main_peers():
    x, z, yh, mp = coords()
    dp = dp_of(x, z, yh)
    return dict(
        core=(dp, mp + 1 - 2 * (mp % 2)),
        lo=(dp, (mp + 2) % 4),
        cross=(dp, 3 - mp),
        hi=(dp + 1 - 2 * (dp % 2), (mp + 2) % 4),
        xp=(dp_of((x + 1) % 4, z, yh), mp),
        xm=(dp_of((x + 3) % 4, z, yh), mp),
        zp=(dp_of(x, (z + 1) % 8, yh), mp),
        zm=(dp_of(x, (z + 7) % 8, yh), mp),
    )


def gelu(u):
    inner = u * (0.7978845608028654 + 0.035677408136300125 * (u * u))
    half = 0.5 * u
    return half + half * jnp.tanh(inner)


def main_kernel(
    patch_ref, inner_ref, outer_ref, inner_tail, outer_tail, text_ref, counts_ref, pair_ref, scale_ref, bias_ref,
    loss_ref, emb_ref, txt_ref,
    w1_own, w2_own, w1_oth, w2_oth, xin, xres, xn, acc, hid, part_out, part_in,
    load_sem, own_sem, patch_send, patch_recv, norm_send, norm_recv, y_send, y_recv,
    side_send, side_recv, part_send, part_recv, *tail_refs,
):
    x, z, yh, mp = coords()
    dp = dp_of(x, z, yh)
    core = mp % 2
    colour = [(x + 2 * z) % 4, (2 * x + z) % 4]
    peers = main_peers()
    barrier = pltpu.get_barrier_semaphore()
    group, line, plane = tail_peers()
    everyone = [peers["hi"]] + group + line + plane
    for peer in everyone:
        pl.semaphore_signal(barrier, inc=1, device_id=peer, device_id_type=MESH)
    mains = pl.ds(2 * TAIL, MAIN)
    loads = [
        pltpu.make_async_copy(inner_ref.at[pl.ds(0, MAIN)], w1_own.at[mains], load_sem.at[0]),
        pltpu.make_async_copy(outer_ref.at[pl.ds(0, MAIN)], w2_own.at[mains], load_sem.at[1]),
    ]
    mine = [
        pltpu.make_async_copy(
            patch_ref.at[:, pl.ds(pl.multiple_of(ROWS * mp + 128 * rb, 128), 128)], xin.at[rb, mp], own_sem.at[rb])
        for rb in range(4)]
    for copy in mine + loads:
        copy.start()
    live = lax.broadcasted_iota(jnp.int32, (TAIL, 1), 0) < inner_ref.shape[0] - MAIN
    for tail_ref, own, oth in ((inner_tail, w1_own, w1_oth), (outer_tail, w2_own, w2_oth)):
        value = jnp.where(live, tail_ref[...].astype(F32), 0.0).astype(BF16)
        own[0:TAIL, :] = value
        oth[TAIL:2 * TAIL, :] = value
    tail = Tail(text_ref, counts_ref, pair_ref, scale_ref, bias_ref, loss_ref, emb_ref, txt_ref, *tail_refs)
    tail.begin()
    pl.semaphore_wait(barrier, len(everyone))

    def patch_copies(rb):
        return [pltpu.make_async_remote_copy(
            src_ref=patch_ref.at[:, pl.ds(pl.multiple_of(ROWS * ((mp + k) % 4) + 128 * rb, 128), 128)],
            dst_ref=xin.at[rb, mp],
            send_sem=patch_send.at[rb, k - 1], recv_sem=patch_recv.at[rb, k - 1],
            device_id=(dp, (mp + k) % 4), device_id_type=MESH) for k in range(1, 4)]

    def place(stage, k):
        if stage == 0:
            rows = pl.ds(pl.multiple_of(colour[k] * 16, 16), 16)
            return (w1_own, w2_own)[k].at[rows], (w1_oth, w2_oth)[k].at[rows]
        src, dst = (inner_ref, w1_oth) if stage < 5 else (outer_ref, w2_oth)
        first = 256 * ((stage - 1) % 4) + 128 * k + colour[k] * 32
        return src.at[pl.ds(pl.multiple_of(first, 32), 32)], dst.at[pl.ds(pl.multiple_of(first + 128, 32), 32)]

    def y_copy(stage, k):
        src, dst = place(stage, k)
        return pltpu.make_async_remote_copy(
            src_ref=src, dst_ref=dst, send_sem=y_send.at[stage, k], recv_sem=y_recv.at[stage, k],
            device_id=peers["hi" if (stage, k) in HI else "lo"], device_id_type=MESH)

    def side_copies(stage, k):
        near, far = (("xp", "xm"), ("zp", "zm")) if k == 0 else (("zp", "zm"), ("xp", "xm"))
        _, at = place(stage, k)
        return [pltpu.make_async_remote_copy(
            src_ref=at, dst_ref=at, send_sem=side_send.at[stage, k, j], recv_sem=side_recv.at[stage, k, j],
            device_id=peers[who], device_id_type=MESH) for j, who in enumerate((near[0], near[1], far[stage % 2]))]

    queues = {"hi": list(HI), "lo": list(LO)}

    def issue(link):
        if queues[link]:
            item = queues[link].pop(0)
            for copy in patch_copies(item[1]) if item[0] == "P" else [y_copy(*item)]:
                copy.start()

    def forward(stage, k):
        copy = y_copy(stage, k)
        copy.wait_recv()
        for side in side_copies(stage, k):
            side.start()
        copy.wait_send()
        issue("hi" if (stage, k) in HI else "lo")

    arrived = set()

    def arrive(stage):
        if stage not in arrived:
            arrived.add(stage)
            for k in range(2):
                for copy in side_copies(stage, k):
                    copy.wait_recv()

    def norm_copy(rb):
        at = (rb // 2, (rb % 2) * 2 + core)
        return pltpu.make_async_remote_copy(
            src_ref=xn.at[at], dst_ref=xn.at[at], send_sem=norm_send.at[rb], recv_sem=norm_recv.at[rb],
            device_id=peers["core"], device_id_type=MESH)

    def normalise(rb):
        mine[rb].wait()
        for copy in patch_copies(rb):
            copy.wait_recv()
        issue("lo")
        raw = xin[rb].reshape(D, 128)
        wide = raw.astype(F32)
        wide = wide - jnp.sum(wide, axis=0, keepdims=True) * (1.0 / D)
        spread = jnp.sum(wide * wide, axis=0, keepdims=True) * (1.0 / D)
        xn[rb // 2, (rb % 2) * 2 + core] = (wide * lax.rsqrt(spread + epsilon)).astype(BF16).T
        norm_copy(rb).start()
        xres[rb] = raw.T

    def expand(half, weights, lo, hi):
        hid[half, :, lo:hi] = gelu(lax.dot_general(
            xn[half].reshape(512, D), weights[lo:hi, :], (((1,), (1,)), ((), ())), preferred_element_type=F32)).astype(BF16)

    def own_expand(half, j):
        if j == 0:
            norm_copy(2 * half).wait_recv()
            norm_copy(2 * half + 1).wait_recv()
            if half == 0:
                loads[0].wait()
        expand(half, w1_own, 128 + 256 * j, 384 + 256 * j)

    def mix(half, weights, lo, hi, left, right, fresh):
        term = jnp.dot(
            hid[half, :, lo:hi], weights[lo:hi, left:right], preferred_element_type=F32).reshape(4, 128, right - left)
        acc[half, :, :, left:right] = term if fresh else acc[half, :, :, left:right] + term

    def own_mix(half, n):
        if half == 0 and n == 0:
            loads[1].wait()
        mix(half, w2_own, 128, 1152, (0, 640)[n], (640, 1152)[n], True)

    def other_expand(half, j):
        arrive(j)
        expand(half, w1_oth, 256 * j - 128 if j else 0, 256 * j + 128)

    def other_mix(half, n):
        arrive(5)
        arrive(6)
        mix(half, w2_oth, 0, 640, (0, 640)[n], (640, 1152)[n], False)

    def part_copy(rb):
        return pltpu.make_async_remote_copy(
            src_ref=part_out.at[rb], dst_ref=part_in.at[rb], send_sem=part_send.at[rb],
            recv_sem=part_recv.at[rb], device_id=peers["core"], device_id_type=MESH)

    def last_mix(half):
        arrive(7)
        arrive(8)
        mix(half, w2_oth, 640, 1152, 0, D, False)
        for r in range(2):
            rb = half * 2 + r
            part_out[rb] = acc[half, 2 * r + 1 - core].astype(BF16)
            part_copy(rb).start()

    tail.greet()
    for _ in range(WINDOW):
        issue("hi")
        issue("lo")
    steps = dict(
        F=forward, N=normalise, E=own_expand, M=own_mix, H=other_expand, A=other_mix, B=last_mix)
    texts = {2: tail.text_line, 20: tail.text_plane, 46: tail.text_done}
    for at, (name, *where) in enumerate(ORDER):
        steps[name](*where)
        if at in texts:
            texts[at]()

    n0 = counts_ref[0]
    n1 = n0 + counts_ref[1]

    def finish(rb, totals):
        part_copy(rb).wait_recv()
        value = xres[rb].astype(F32) + (acc[rb // 2, (rb % 2) * 2 + core] + part_in[rb].astype(F32))
        shifted = value - jnp.sum(value, axis=1, keepdims=True) * (1.0 / D)
        spread = jnp.sum(shifted * shifted, axis=1, keepdims=True) * (1.0 / D)
        scale = lax.rsqrt(spread + epsilon)
        ids = ROWS * mp + 128 * rb + lax.broadcasted_iota(jnp.int32, (128, 1), 0)
        normed = shifted * scale
        a = jnp.sum(jnp.where(ids < n0, normed, 0.0), axis=0, keepdims=True)
        b = jnp.sum(jnp.where((ids >= n0) & (ids < n1), normed, 0.0), axis=0, keepdims=True)
        return totals[0] + a, totals[1] + b
    zero = jnp.zeros((1, D), F32)
    a, b = lax.fori_loop(0, 4, finish, (zero, zero))
    tail.image_line(a, b)
    tail.image_rows()

    def drain():
        for rb in range(4):
            for copy in patch_copies(rb):
                copy.wait_send()
            norm_copy(rb).wait_send()
            part_copy(rb).wait_send()
        for stage in range(STAGES):
            for k in range(2):
                for copy in side_copies(stage, k):
                    copy.wait_send()
    tail.end(drain)


def main_scratch():
    dma = pltpu.SemaphoreType.DMA
    return [
        pltpu.VMEM((D, D), BF16), pltpu.VMEM((D, D), BF16), pltpu.VMEM((D, D), BF16), pltpu.VMEM((D, D), BF16),
        pltpu.VMEM((4, 4, DL, 128), BF16), pltpu.VMEM((4, 128, D), BF16),
        pltpu.VMEM((2, 4, 128, D), BF16), pltpu.VMEM((2, 4, 128, D), F32),
        pltpu.VMEM((2, 512, D), BF16),
        pltpu.VMEM((4, 128, D), BF16), pltpu.VMEM((4, 128, D), BF16),
        dma((2,)), dma((4,)), dma((4, 3)), dma((4, 3)), dma((4,)), dma((4,)), dma((STAGES, 2)), dma((STAGES, 2)),
        dma((STAGES, 2, 3)), dma((STAGES, 2, 3)), dma((4,)), dma((4,)),
    ]


def hand_over(loss_ref, emb_ref, txt_ref, loss_out, emb_out, txt_out):
    emb_out[...] = emb_ref[...]
    txt_out[...] = txt_ref[...]
    loss_out[0] = loss_ref[0, 0]
    loss_out[1] = loss_ref[1, 0]


def shards(
    patches, counts, pair_ids, inner_weight, outer_weight, text_embed, log_scale, logit_bias
):
    vmem, smem = pl.BlockSpec(memory_space=pltpu.VMEM), pl.BlockSpec(memory_space=pltpu.SMEM)
    hbm = pl.BlockSpec(memory_space=pl.ANY)
    end = pl.BlockSpec((TAIL, D), lambda i: (MAIN // TAIL, 0))
    half = jax.ShapeDtypeStruct((2, DL), F32)
    inner = inner_weight.T
    found = pl.pallas_call(
        main_kernel,
        grid=(1,),
        out_shape=(jax.ShapeDtypeStruct((2, 128), F32), half, half),
        in_specs=[hbm, hbm, hbm, end, end, vmem, smem, smem, smem, smem],
        out_specs=(vmem, vmem, vmem),
        scratch_shapes=main_scratch() + tail_scratch(),
        compiler_params=pltpu.CompilerParams(
            collective_id=1, has_side_effects=True, vmem_limit_bytes=56 * 2**20),
        name="tower",
    )(patches.T, inner, outer_weight, inner, outer_weight, text_embed, counts, pair_ids, log_scale, logit_bias)
    return pl.pallas_call(
        hand_over,
        out_shape=(jax.ShapeDtypeStruct((2,), F32), half, half),
        in_specs=[vmem, vmem, vmem],
        out_specs=(smem, vmem, vmem),
        name="hand_over",
    )(*found)


def solution(mesh):
    placed = (
        P("dp", "mp"),
        P("dp"),
        P("dp"),
        P(None, "mp"),
        P("mp", None),
        P("dp", "mp"),
        P(),
        P(),
    )
    return jax.shard_map(
        shards,
        mesh=mesh,
        in_specs=placed,
        out_specs=(P("dp"), P("dp", "mp"), P("dp", "mp")),
        check_vma=False,
    )
```

```python
import functools

import jax
import jax.numpy as jnp
from jax import lax
from jax.experimental import pallas as pl
from jax.experimental.pallas import tpu as pltpu
from jax.sharding import PartitionSpec as P

MESH = pl.DeviceIdType.MESH
epsilon = 1e-06
D = 1152
DL = 288
F32, BF16 = jnp.float32, jnp.bfloat16


def coords():
    dp, mp = lax.axis_index("dp"), lax.axis_index("mp")
    return dp // 16, (dp // 2) % 8, dp % 2, mp


def dp_of(x, z, yh):
    return x * 16 + z * 2 + yh


def tail_peers():
    x, z, yh, mp = coords()
    dp = dp_of(x, z, yh)
    group = [(dp, (mp + k) % 4) for k in range(1, 4)]
    line = [(dp_of(x, (z + k) % 8, yh), mp) for k in range(1, 8)]
    plane = [(dp_of((x + k // 2) % 4, z, (yh + k) % 2), mp) for k in range(1, 8)]
    return group, line, plane


def by_parity(column, even, odd):
    return jnp.where(column % 2 == 0, even, odd)


def parity_sums(values):
    own = jnp.sum(values, axis=1, keepdims=True)
    row = lax.broadcasted_iota(jnp.int32, own.shape, 0)
    even = jnp.sum(jnp.where(row % 2 == 0, own, 0.0), axis=0, keepdims=True)
    odd = jnp.sum(jnp.where(row % 2 == 1, own, 0.0), axis=0, keepdims=True)
    return even, odd


def three_terms(values):
    high = values.astype(BF16).astype(F32)
    rest = values - high
    mid = rest.astype(BF16).astype(F32)
    return jnp.concatenate([high, mid, rest - mid], axis=0).astype(BF16)


def stacked(wide):
    return jnp.concatenate([wide[:, 128 * q:128 * q + 128] for q in range(4)], axis=0)


def folded(dots):
    return dots[0:2] + pltpu.roll(dots, 512 - 2, 1)[2:4] + pltpu.roll(dots, 512 - 4, 1)[4:6]


class Tail:
    def __init__(self, text_ref, counts_ref, pair_ref, scale_ref, bias_ref, loss_ref, emb_ref, txt_ref,
                 psum, tss, wide, units, tline, iline, tall, iall, pairs, dots, *sems):
        self.__dict__.update(locals())
        self.x, self.z, self.yh, self.mp = coords()
        self.dp = dp_of(self.x, self.z, self.yh)
        self.own_line = self.x * 2 + self.yh
        self.group, self.line, self.plane = tail_peers()
        self.copies = {}

    def send(self, name, sem, ref, peers):
        sent, got = self.sems[2 * sem], self.sems[2 * sem + 1]
        self.copies[name] = [pltpu.make_async_remote_copy(
            src_ref=ref, dst_ref=ref, send_sem=sent.at[k], recv_sem=got.at[k],
            device_id=peer, device_id_type=MESH) for k, peer in enumerate(peers)]
        for copy in self.copies[name]:
            copy.start()

    def take(self, name):
        for copy in self.copies[name]:
            copy.wait_recv()

    def begin(self):
        text = self.text_ref[...].astype(F32)
        self.tss[self.mp] = jnp.zeros((8, 128), F32)
        self.tss[self.mp, 0:2, :] = jnp.broadcast_to(jnp.sum(text * text, axis=1, keepdims=True), (2, 128))
        self.units[...] = jnp.zeros((4, 8, 128), F32)
        for b in range(3):
            width = 128 if b < 2 else DL - 256
            self.units[0, 2 * b:2 * b + 2, 0:width] = text[:, 128 * b:128 * b + width]
        self.wide[...] = jnp.zeros((8, D + 128), F32)

    def greet(self):
        self.send("tss", 0, self.tss.at[self.mp], self.group)

    def text_line(self):
        self.take("tss")
        total = ((self.tss[0] + self.tss[1]) + self.tss[2]) + self.tss[3]
        norm = lax.rsqrt(total + epsilon)
        row = lax.broadcasted_iota(jnp.int32, (8, 128), 0)
        norm = by_parity(row, norm[0:1], norm[1:2])
        unit = self.units[0] * norm
        self.units[0] = unit
        self.units[1] = norm
        wire = unit.astype(BF16).astype(F32)
        ids = jnp.where(row == 6, self.pair_ref[0], self.pair_ref[1]).astype(F32)
        self.tline[self.z] = jnp.where(row < 6, wire, ids)
        self.send("tline", 1, self.tline.at[self.z], self.line)

    def text_plane(self):
        self.take("tline")
        self.tall[self.own_line] = self.tline[...].reshape(64, 128).astype(BF16)
        self.send("tplane", 2, self.tall.at[self.own_line], self.plane)

    def text_done(self):
        self.take("tplane")
        first = (lax.broadcasted_iota(jnp.int32, (16, 128), 1) == 0).astype(F32).astype(BF16)
        column = lax.dot_general(
            first, self.tall[...].reshape(512, 128), (((1,), (1,)), ((), ())), preferred_element_type=F32)
        self.pairs[...] = pltpu.roll(stacked(column[0:2]), 128 - 4, 1)

    def image_line(self, first, second):
        self.psum[self.mp, 0:1, :] = first
        self.psum[self.mp, 1:2, :] = second
        self.send("psum", 3, self.psum.at[self.mp], self.group)

    def image_rows(self):
        self.take("psum")
        psum, mp = self.psum, self.mp
        row = lax.broadcasted_iota(jnp.int32, (2, 1), 0)
        count = jnp.where(row == 0, self.counts_ref[0], self.counts_ref[1]).astype(F32)
        pooled = (((psum[0] + psum[1]) + psum[2]) + psum[3]) / count
        norm = lax.rsqrt(jnp.sum(pooled * pooled, axis=1, keepdims=True) + epsilon)
        self.wide[0:2, :D] = pooled * norm
        lane = lax.broadcasted_iota(jnp.int32, (2, 128), 1)
        for b in range(3):
            block = self.wide[0:2, 128 * b:128 * b + 128]
            for k in range(1, 4):
                block = jnp.where(mp == k, self.wide[0:2, DL * k + 128 * b:DL * k + 128 * b + 128], block)
            self.units[2, 2 * b:2 * b + 2, :] = block if b < 2 else jnp.where(lane < DL - 256, block, 0.0)
        row8 = lax.broadcasted_iota(jnp.int32, (8, 128), 0)
        unit = self.units[2]
        self.units[3] = by_parity(row8, norm[0:1], norm[1:2]) + jnp.zeros((8, 128), F32)
        wire = unit.astype(BF16).astype(F32)
        self.iline[self.z] = wire
        self.send("iline", 4, self.iline.at[self.z], self.line)

    def left(self, unit):
        wire = unit.astype(BF16).astype(F32)
        return jnp.concatenate([wire, unit - wire], axis=0).astype(BF16)

    def against(self, unit, everyone):
        found = lax.dot_general(
            self.left(unit), everyone, (((1,), (1,)), ((), ())), preferred_element_type=F32)
        return folded(found[0:8]), folded(found[8:16])

    def end(self, meanwhile):
        texts = self.tall[...].reshape(512, 128)
        image, image_rest = self.against(self.units[2], texts)
        self.take("iline")
        self.iall[self.own_line] = self.iline[...].reshape(64, 128).astype(BF16)
        self.send("iplane", 5, self.iall.at[self.own_line], self.plane)
        meanwhile()
        self.take("iplane")
        images = self.iall[...].reshape(512, 128)
        text, text_rest = self.against(self.units[0], images)
        kind = lax.broadcasted_iota(jnp.int32, (2, 512), 1) % 8
        mixed = jnp.where(kind < 2, image, jnp.where(
            kind < 4, pltpu.roll(text, 2, 1), jnp.where(
                kind < 6, pltpu.roll(image_rest, 4, 1), pltpu.roll(text_rest, 6, 1))))
        self.dots[self.mp] = stacked(mixed)
        self.send("dots", 6, self.dots.at[self.mp], self.group)
        row = lax.broadcasted_iota(jnp.int32, (8, 128), 0)
        lane = lax.broadcasted_iota(jnp.int32, (8, 128), 1)
        column = (row // 2) * 128 + lane
        kind = column % 8
        place = column // 64
        shard = (place // 2) * 16 + ((column // 8) % 8) * 2 + place % 2
        other = shard * 2 + kind % 2
        own = row % 2
        own_pair = by_parity(row, self.pair_ref[0], self.pair_ref[1])
        match = jnp.where(kind < 2, own_pair, self.pairs[...].astype(jnp.int32)) == jnp.where(
            kind < 2, other, self.dp * 2 + own)
        label = jnp.where(match, 1.0, -1.0)
        scale = jnp.exp(jnp.full((8, 128), self.scale_ref[0], F32))
        self.take("dots")
        dots = self.dots
        dot = ((dots[0] + dots[1]) + dots[2]) + dots[3]
        turned = -label * (scale * dot + self.bias_ref[0])
        small = jnp.exp(-jnp.abs(turned))
        soft = jnp.where(kind < 2, jnp.maximum(turned, 0.0) + jnp.log1p(small), 0.0)
        sigmoid = jnp.where(turned >= 0, 1.0, small) / (1.0 + small)
        slope = jnp.where(kind < 4, -label * sigmoid, 0.0)
        term = scale * slope * (dot + pltpu.roll(dot, 128 - 4, 1))
        loss = parity_sums(soft)
        image_proj = parity_sums(jnp.where(kind < 2, term, 0.0))
        text_proj = parity_sums(jnp.where(kind >= 2, term, 0.0))
        blank = jnp.zeros((2, 512), F32)
        for everyone, kept, proj, at, out in (
            (texts, kind < 2, image_proj, 2, self.emb_ref), (images, kind >= 2, text_proj, 0, self.txt_ref)
        ):
            flat = jnp.where(kept, slope, 0.0)
            flat = jnp.concatenate([flat[2 * q:2 * q + 2] for q in range(4)], axis=1)
            if at == 0:
                flat = pltpu.roll(flat, 512 - 2, 1)
            spread = jnp.concatenate([flat, pltpu.roll(flat, 2, 1), pltpu.roll(flat, 4, 1), blank], axis=0)
            found = jnp.dot(three_terms(spread), everyone, preferred_element_type=F32)
            direction = (found[0:8] + (found[8:16] + found[16:24])) * scale
            grad = (direction - self.units[at] * by_parity(row, proj[0], proj[1])) * self.units[at + 1]
            for b in range(3):
                width = 128 if b < 2 else DL - 256
                out[:, 128 * b:128 * b + width] = grad[2 * b:2 * b + 2, 0:width]
        self.loss_ref[...] = by_parity(lax.broadcasted_iota(jnp.int32, (2, 128), 0), loss[0], loss[1])
        for copies in self.copies.values():
            for copy in copies:
                copy.wait_send()


def tail_scratch():
    dma = pltpu.SemaphoreType.DMA
    pair = lambda n: [dma((n,)), dma((n,))]
    return [
        pltpu.VMEM((4, 2, D), F32), pltpu.VMEM((4, 8, 128), F32), pltpu.VMEM((8, D + 128), F32),
        pltpu.VMEM((4, 8, 128), F32), pltpu.VMEM((8, 8, 128), F32), pltpu.VMEM((8, 8, 128), F32),
        pltpu.VMEM((8, 64, 128), BF16), pltpu.VMEM((8, 64, 128), BF16), pltpu.VMEM((8, 128), F32),
        pltpu.VMEM((4, 8, 128), F32),
    ] + pair(3) + pair(7) + pair(7) + pair(3) + pair(7) + pair(7) + pair(3)


ROWS = 512
MAIN = 1024
TAIL = 64
UNITS = 1076
WINDOW = 6
STAGES = 9
HI = [(1, 0), (2, 0), (2, 1), (0, 0), (0, 1), (3, 0), (3, 1), (4, 1), (5, 1), (6, 0), (6, 1), (8, 0)]
LO = [('P', 0), ('P', 1), (1, 1), ('P', 2), (4, 0), ('P', 3), (5, 0), (7, 0), (7, 1), (8, 1)]
ORDER = [('F', 1, 0), ('F', 2, 0), ('N', 0), ('F', 2, 1), ('e', 0, 0), ('F', 0, 0), ('e', 0, 1), ('F', 0, 1), ('N', 1), ('m', 0), ('F', 3, 0), ('F', 1, 1), ('e', 1, 0), ('e', 1, 1), ('F', 3, 1), ('m', 1), ('H', 0, 0), ('H', 0, 2), ('F', 4, 1), ('N', 2), ('F', 4, 0), ('F', 5, 1), ('H', 0, 1), ('F', 6, 0), ('H', 0, 3), ('F', 6, 1), ('N', 3), ('H', 0, 4), ('F', 5, 0), ('F', 8, 0), ('E', 1, 0), ('E', 1, 1), ('E', 1, 2), ('F', 7, 0), ('E', 1, 3), ('M', 1, 0), ('F', 7, 1), ('M', 1, 1), ('H', 1, 0), ('H', 1, 1), ('F', 8, 1), ('H', 1, 2), ('H', 1, 3), ('H', 1, 4), ('A', 0, 0), ('A', 0, 1), ('A', 1, 0), ('A', 1, 1), ('B', 0), ('B', 1)]


def main_peers():
    x, z, yh, mp = coords()
    dp = dp_of(x, z, yh)
    return dict(
        core=(dp, mp + 1 - 2 * (mp % 2)),
        lo=(dp, (mp + 2) % 4),
        cross=(dp, 3 - mp),
        hi=(dp + 1 - 2 * (dp % 2), (mp + 2) % 4),
        xp=(dp_of((x + 1) % 4, z, yh), mp),
        xm=(dp_of((x + 3) % 4, z, yh), mp),
        zp=(dp_of(x, (z + 1) % 8, yh), mp),
        zm=(dp_of(x, (z + 7) % 8, yh), mp),
    )


def gelu(u):
    inner = u * (0.7978845608028654 + 0.035677408136300125 * (u * u))
    half = 0.5 * u
    return half + half * jnp.tanh(inner)


def main_kernel(
    patch_ref, inner_ref, outer_ref, text_ref, counts_ref, pair_ref, scale_ref, bias_ref,
    loss_ref, emb_ref, txt_ref,
    w1_own, w2_own, tails, w1_oth, w2_oth, xin, xres, xn, acc, hid, part_out, part_in,
    load_sem, own_sem, patch_send, patch_recv, norm_send, norm_recv, y_send, y_recv,
    side_send, side_recv, part_send, part_recv, heard, *tail_refs,
):
    x, z, yh, mp = coords()
    dp = dp_of(x, z, yh)
    core = mp % 2
    colour = [(x + 2 * z) % 4, (2 * x + z) % 4]
    peers = main_peers()
    barrier = pltpu.get_barrier_semaphore()
    for peer in peers.values():
        pl.semaphore_signal(barrier, inc=1, device_id=peer, device_id_type=MESH)
    loads = [
        pltpu.make_async_copy(inner_ref, w1_own, load_sem.at[0]),
        pltpu.make_async_copy(outer_ref, w2_own, load_sem.at[1]),
    ]
    mine = [
        pltpu.make_async_copy(
            patch_ref.at[:, pl.ds(pl.multiple_of(ROWS * mp + 128 * rb, 128), 128)], xin.at[rb, mp], own_sem.at[rb])
        for rb in range(4)]
    for copy in mine + loads:
        copy.start()
    tail = Tail(text_ref, counts_ref, pair_ref, scale_ref, bias_ref, loss_ref, emb_ref, txt_ref, *tail_refs)
    tail.begin()
    pl.semaphore_wait(barrier, len(peers))

    def patch_copies(rb):
        return [pltpu.make_async_remote_copy(
            src_ref=patch_ref.at[:, pl.ds(pl.multiple_of(ROWS * ((mp + k) % 4) + 128 * rb, 128), 128)],
            dst_ref=xin.at[rb, mp],
            send_sem=patch_send.at[rb, k - 1], recv_sem=patch_recv.at[rb, k - 1],
            device_id=(dp, (mp + k) % 4), device_id_type=MESH) for k in range(1, 4)]

    def place(stage, k):
        if stage == 0:
            rows = pl.ds(pl.multiple_of(colour[k] * 16, 16), 16)
            return tails.at[k, rows], (w1_oth, w2_oth)[k].at[rows]
        src, dst = (inner_ref, w1_oth) if stage < 5 else (outer_ref, w2_oth)
        first = 256 * ((stage - 1) % 4) + 128 * k + colour[k] * 32
        return src.at[pl.ds(pl.multiple_of(first, 32), 32)], dst.at[pl.ds(pl.multiple_of(first + 128, 32), 32)]

    def y_copy(stage, k):
        src, dst = place(stage, k)
        return pltpu.make_async_remote_copy(
            src_ref=src, dst_ref=dst, send_sem=y_send.at[stage, k], recv_sem=y_recv.at[stage, k],
            device_id=peers["hi" if (stage, k) in HI else "lo"], device_id_type=MESH)

    def side_copies(stage, k):
        near, far = (("xp", "xm"), ("zp", "zm")) if k == 0 else (("zp", "zm"), ("xp", "xm"))
        _, at = place(stage, k)
        return [pltpu.make_async_remote_copy(
            src_ref=at, dst_ref=at, send_sem=side_send.at[stage, k, j], recv_sem=side_recv.at[stage, k, j],
            device_id=peers[who], device_id_type=MESH) for j, who in enumerate((near[0], near[1], far[stage % 2]))]

    queues = {"hi": list(HI), "lo": list(LO)}

    def issue(link):
        if queues[link]:
            item = queues[link].pop(0)
            for copy in patch_copies(item[1]) if item[0] == "P" else [y_copy(*item)]:
                copy.start()

    def forward(stage, k):
        copy = y_copy(stage, k)
        copy.wait_recv()
        for side in side_copies(stage, k):
            side.start()
        issue("hi" if (stage, k) in HI else "lo")

    arrived = set()

    def arrive(stage):
        if stage not in arrived:
            arrived.add(stage)
            for k in range(2):
                for copy in side_copies(stage, k):
                    copy.wait_recv()

    def norm_copy(rb):
        at = (rb // 2, (rb % 2) * 2 + core)
        return pltpu.make_async_remote_copy(
            src_ref=xn.at[at], dst_ref=xn.at[at], send_sem=norm_send.at[rb], recv_sem=norm_recv.at[rb],
            device_id=peers["core"], device_id_type=MESH)

    def normalise(rb):
        mine[rb].wait()
        for copy in patch_copies(rb):
            copy.wait_recv()
        issue("lo")
        raw = xin[rb].reshape(D, 128)
        wide = raw.astype(F32)
        wide = wide - jnp.sum(wide, axis=0, keepdims=True) * (1.0 / D)
        spread = jnp.sum(wide * wide, axis=0, keepdims=True) * (1.0 / D)
        xn[rb // 2, (rb % 2) * 2 + core] = (wide * lax.rsqrt(spread + epsilon)).astype(BF16).T
        norm_copy(rb).start()
        xres[rb] = raw.T

    def expand(rows, weights, lo, hi):
        return gelu(lax.dot_general(
            rows, weights[lo:hi, :], (((1,), (1,)), ((), ())), preferred_element_type=F32)).astype(BF16)

    def quarter_expand(rb, n):
        if n == 0:
            norm_copy(rb).wait_recv()
        for j in (2 * n, 2 * n + 1):
            hid[0, 256 * rb:256 * rb + 256, 128 + 256 * j:384 + 256 * j] = expand(
                xn[0, 2 * rb:2 * rb + 2].reshape(256, D), w1_own, 256 * j, 256 * j + 256)

    def quarter_mix(rb):
        acc[0, 2 * rb:2 * rb + 2] = jnp.dot(
            hid[0, 256 * rb:256 * rb + 256, 128:1152], w2_own[0:MAIN, :], preferred_element_type=F32).reshape(2, 128, D)

    def own_expand(half, j):
        if j == 0:
            norm_copy(2 * half).wait_recv()
            norm_copy(2 * half + 1).wait_recv()
        hid[half, :, 128 + 256 * j:384 + 256 * j] = expand(
            xn[half].reshape(512, D), w1_own, 256 * j, 256 * j + 256)

    def mix(half, weights, lo, hi, left, right):
        return jnp.dot(
            hid[half, :, lo:hi], weights[:, left:right], preferred_element_type=F32).reshape(4, 128, right - left)

    def own_mix(half, n):
        left, right = ((0, 640), (640, 1152))[n]
        acc[half, :, :, left:right] = mix(half, w2_own.at[0:MAIN], 128, 1152, left, right)

    def other_expand(half, j):
        arrive(j)
        lo, hi = 256 * j - 128 if j else 0, 256 * j + 128
        hid[half, :, lo:hi] = expand(xn[half].reshape(512, D), w1_oth, lo, hi)

    def other_mix(half, n):
        arrive(5)
        arrive(6)
        left, right = ((0, 640), (640, 1152))[n]
        acc[half, :, :, left:right] += mix(half, w2_oth.at[0:640], 0, 640, left, right)

    def part_copy(rb):
        return pltpu.make_async_remote_copy(
            src_ref=part_out.at[rb], dst_ref=part_in.at[rb], send_sem=part_send.at[rb],
            recv_sem=part_recv.at[rb], device_id=peers["core"], device_id_type=MESH)

    def last_mix(half):
        arrive(7)
        arrive(8)
        acc[half] += mix(half, w2_oth.at[640:1152], 640, 1152, 0, D)
        for r in range(2):
            rb = half * 2 + r
            part_out[rb] = acc[half, 2 * r + 1 - core].astype(BF16)
            part_copy(rb).start()

    tail.greet()
    for _ in range(2):
        issue("hi")
        issue("lo")
    kept = inner_ref.shape[0] - MAIN
    for k, (own, oth) in enumerate(((w1_own, w1_oth), (w2_own, w2_oth))):
        loads[k].wait()
        value, blank = own[MAIN:MAIN + kept, :], jnp.zeros((TAIL - kept, D), BF16)
        tails[k, 0:kept, :] = value
        tails[k, kept:TAIL, :] = blank
        oth[TAIL:TAIL + kept, :] = value
        oth[TAIL + kept:2 * TAIL, :] = blank
    for _ in range(WINDOW - 2):
        issue("hi")
        issue("lo")
    steps = dict(
        F=forward, N=normalise, e=quarter_expand, m=quarter_mix, E=own_expand, M=own_mix, H=other_expand, A=other_mix, B=last_mix)

    beside = [peers[name] for name in ("lo", "hi", "xp", "xm", "zp", "zm")]

    def tell(n):
        for peer in beside:
            pl.semaphore_signal(heard.at[n], inc=1, device_id=peer, device_id_type=MESH)

    def hear(n):
        pl.semaphore_wait(heard.at[n], len(beside))
        if n < 2:
            tell(n + 1)
    tell(0)
    texts = {4: lambda: hear(0), 8: lambda: hear(1), 12: lambda: (hear(2), tail.text_line()),
             26: tail.text_plane, 48: tail.text_done}
    for at, (name, *where) in enumerate(ORDER):
        steps[name](*where)
        if at in texts:
            texts[at]()

    n0 = counts_ref[0]
    n1 = n0 + counts_ref[1]

    def finish(rb, totals):
        part_copy(rb).wait_recv()
        value = xres[rb].astype(F32) + (acc[rb // 2, (rb % 2) * 2 + core] + part_in[rb].astype(F32))
        shifted = value - jnp.sum(value, axis=1, keepdims=True) * (1.0 / D)
        spread = jnp.sum(shifted * shifted, axis=1, keepdims=True) * (1.0 / D)
        scale = lax.rsqrt(spread + epsilon)
        ids = ROWS * mp + 128 * rb + lax.broadcasted_iota(jnp.int32, (128, 1), 0)
        normed = shifted * scale
        a = jnp.sum(jnp.where(ids < n0, normed, 0.0), axis=0, keepdims=True)
        b = jnp.sum(jnp.where((ids >= n0) & (ids < n1), normed, 0.0), axis=0, keepdims=True)
        return totals[0] + a, totals[1] + b
    zero = jnp.zeros((1, D), F32)
    a, b = lax.fori_loop(0, 4, finish, (zero, zero))
    tail.image_line(a, b)
    tail.image_rows()

    def drain():
        for rb in range(4):
            for copy in patch_copies(rb):
                copy.wait_send()
            norm_copy(rb).wait_send()
            part_copy(rb).wait_send()
        for stage in range(STAGES):
            for k in range(2):
                for copy in [y_copy(stage, k)] + side_copies(stage, k):
                    copy.wait_send()
    tail.end(drain)


def main_scratch():
    dma = pltpu.SemaphoreType.DMA
    return [
        pltpu.VMEM((UNITS, D), BF16), pltpu.VMEM((UNITS, D), BF16), pltpu.VMEM((2, TAIL, D), BF16),
        pltpu.VMEM((D, D), BF16), pltpu.VMEM((D, D), BF16),
        pltpu.VMEM((4, 4, DL, 128), BF16), pltpu.VMEM((4, 128, D), BF16),
        pltpu.VMEM((2, 4, 128, D), BF16), pltpu.VMEM((2, 4, 128, D), F32),
        pltpu.VMEM((2, 512, D), BF16),
        pltpu.VMEM((4, 128, D), BF16), pltpu.VMEM((4, 128, D), BF16),
        dma((2,)), dma((4,)), dma((4, 3)), dma((4, 3)), dma((4,)), dma((4,)), dma((STAGES, 2)), dma((STAGES, 2)),
        dma((STAGES, 2, 3)), dma((STAGES, 2, 3)), dma((4,)), dma((4,)), pltpu.SemaphoreType.REGULAR((3,)),
    ]


def hand_over(loss_ref, emb_ref, txt_ref, loss_out, emb_out, txt_out):
    emb_out[...] = emb_ref[...]
    txt_out[...] = txt_ref[...]
    loss_out[0] = loss_ref[0, 0]
    loss_out[1] = loss_ref[1, 0]


def shards(
    patches, counts, pair_ids, inner_weight, outer_weight, text_embed, log_scale, logit_bias
):
    vmem, smem = pl.BlockSpec(memory_space=pltpu.VMEM), pl.BlockSpec(memory_space=pltpu.SMEM)
    hbm = pl.BlockSpec(memory_space=pl.ANY)
    half = jax.ShapeDtypeStruct((2, DL), F32)
    found = pl.pallas_call(
        main_kernel,
        out_shape=(jax.ShapeDtypeStruct((2, 128), F32), half, half),
        in_specs=[hbm, hbm, hbm, vmem, smem, smem, smem, smem],
        out_specs=(vmem, vmem, vmem),
        scratch_shapes=main_scratch() + tail_scratch(),
        compiler_params=pltpu.CompilerParams(
            collective_id=1, has_side_effects=True, vmem_limit_bytes=56 * 2**20),
        name="tower",
    )(patches.T, inner_weight.T, outer_weight, text_embed, counts, pair_ids, log_scale, logit_bias)
    return pl.pallas_call(
        hand_over,
        out_shape=(jax.ShapeDtypeStruct((2,), F32), half, half),
        in_specs=[vmem, vmem, vmem],
        out_specs=(smem, vmem, vmem),
        name="hand_over",
    )(*found)


def solution(mesh):
    placed = (
        P("dp", "mp"),
        P("dp"),
        P("dp"),
        P(None, "mp"),
        P("mp", None),
        P("dp", "mp"),
        P(),
        P(),
    )
    return jax.shard_map(
        shards,
        mesh=mesh,
        in_specs=placed,
        out_specs=(P("dp"), P("dp", "mp"), P("dp", "mp")),
        check_vma=False,
    )
```

```python
import functools

import jax
import jax.numpy as jnp
from jax import lax
from jax.experimental import pallas as pl
from jax.experimental.pallas import tpu as pltpu
from jax.sharding import PartitionSpec as P

MESH = pl.DeviceIdType.MESH
epsilon = 1e-06
D = 1152
DL = 288
F32, BF16 = jnp.float32, jnp.bfloat16


def coords():
    dp, mp = lax.axis_index("dp"), lax.axis_index("mp")
    return dp // 16, (dp // 2) % 8, dp % 2, mp


def dp_of(x, z, yh):
    return x * 16 + z * 2 + yh


def tail_peers():
    x, z, yh, mp = coords()
    dp = dp_of(x, z, yh)
    group = [(dp, (mp + k) % 4) for k in range(1, 4)]
    line = [(dp_of(x, (z + k) % 8, yh), mp) for k in range(1, 8)]
    plane = [(dp_of((x + k // 2) % 4, z, (yh + k) % 2), mp) for k in range(1, 8)]
    return group, line, plane


def by_parity(column, even, odd):
    return jnp.where(column % 2 == 0, even, odd)


def parity_sums(values):
    own = jnp.sum(values, axis=1, keepdims=True)
    row = lax.broadcasted_iota(jnp.int32, own.shape, 0)
    even = jnp.sum(jnp.where(row % 2 == 0, own, 0.0), axis=0, keepdims=True)
    odd = jnp.sum(jnp.where(row % 2 == 1, own, 0.0), axis=0, keepdims=True)
    return even, odd


def three_terms(values):
    high = values.astype(BF16).astype(F32)
    rest = values - high
    mid = rest.astype(BF16).astype(F32)
    return jnp.concatenate([high, mid, rest - mid], axis=0).astype(BF16)


def stacked(wide):
    return jnp.concatenate([wide[:, 128 * q:128 * q + 128] for q in range(4)], axis=0)


def folded(dots):
    return dots[0:2] + pltpu.roll(dots, 512 - 2, 1)[2:4] + pltpu.roll(dots, 512 - 4, 1)[4:6]


class Tail:
    def __init__(self, text_ref, counts_ref, pair_ref, scale_ref, bias_ref, loss_ref, emb_ref, txt_ref,
                 psum, tss, wide, units, tline, iline, tall, iall, pairs, dots, *sems):
        self.__dict__.update(locals())
        self.x, self.z, self.yh, self.mp = coords()
        self.dp = dp_of(self.x, self.z, self.yh)
        self.own_line = self.x * 2 + self.yh
        self.group, self.line, self.plane = tail_peers()
        self.copies = {}

    def send(self, name, sem, ref, peers):
        sent, got = self.sems[2 * sem], self.sems[2 * sem + 1]
        self.copies[name] = [pltpu.make_async_remote_copy(
            src_ref=ref, dst_ref=ref, send_sem=sent.at[k], recv_sem=got.at[k],
            device_id=peer, device_id_type=MESH) for k, peer in enumerate(peers)]
        for copy in self.copies[name]:
            copy.start()

    def take(self, name):
        for copy in self.copies[name]:
            copy.wait_recv()

    def begin(self):
        text = self.text_ref[...].astype(F32)
        self.tss[self.mp] = jnp.zeros((8, 128), F32)
        self.tss[self.mp, 0:2, :] = jnp.broadcast_to(jnp.sum(text * text, axis=1, keepdims=True), (2, 128))
        self.units[...] = jnp.zeros((4, 8, 128), F32)
        for b in range(3):
            width = 128 if b < 2 else DL - 256
            self.units[0, 2 * b:2 * b + 2, 0:width] = text[:, 128 * b:128 * b + width]
        self.wide[...] = jnp.zeros((8, D + 128), F32)

    def greet(self):
        self.send("tss", 0, self.tss.at[self.mp], self.group)

    def text_line(self):
        self.take("tss")
        total = ((self.tss[0] + self.tss[1]) + self.tss[2]) + self.tss[3]
        norm = lax.rsqrt(total + epsilon)
        row = lax.broadcasted_iota(jnp.int32, (8, 128), 0)
        norm = by_parity(row, norm[0:1], norm[1:2])
        unit = self.units[0] * norm
        self.units[0] = unit
        self.units[1] = norm
        wire = unit.astype(BF16).astype(F32)
        ids = jnp.where(row == 6, self.pair_ref[0], self.pair_ref[1]).astype(F32)
        self.tline[self.z] = jnp.where(row < 6, wire, ids)
        self.send("tline", 1, self.tline.at[self.z], self.line)

    def text_plane(self):
        self.take("tline")
        self.tall[self.own_line] = self.tline[...].reshape(64, 128).astype(BF16)
        self.send("tplane", 2, self.tall.at[self.own_line], self.plane)

    def text_done(self):
        self.take("tplane")
        first = (lax.broadcasted_iota(jnp.int32, (16, 128), 1) == 0).astype(F32).astype(BF16)
        column = lax.dot_general(
            first, self.tall[...].reshape(512, 128), (((1,), (1,)), ((), ())), preferred_element_type=F32)
        self.pairs[...] = pltpu.roll(stacked(column[0:2]), 128 - 4, 1)

    def image_line(self, first, second):
        self.psum[self.mp, 0:1, :] = first
        self.psum[self.mp, 1:2, :] = second
        self.send("psum", 3, self.psum.at[self.mp], self.group)

    def image_rows(self):
        self.take("psum")
        psum, mp = self.psum, self.mp
        row = lax.broadcasted_iota(jnp.int32, (2, 1), 0)
        count = jnp.where(row == 0, self.counts_ref[0], self.counts_ref[1]).astype(F32)
        pooled = (((psum[0] + psum[1]) + psum[2]) + psum[3]) / count
        norm = lax.rsqrt(jnp.sum(pooled * pooled, axis=1, keepdims=True) + epsilon)
        self.wide[0:2, :D] = pooled * norm
        lane = lax.broadcasted_iota(jnp.int32, (2, 128), 1)
        for b in range(3):
            block = self.wide[0:2, 128 * b:128 * b + 128]
            for k in range(1, 4):
                block = jnp.where(mp == k, self.wide[0:2, DL * k + 128 * b:DL * k + 128 * b + 128], block)
            self.units[2, 2 * b:2 * b + 2, :] = block if b < 2 else jnp.where(lane < DL - 256, block, 0.0)
        row8 = lax.broadcasted_iota(jnp.int32, (8, 128), 0)
        unit = self.units[2]
        self.units[3] = by_parity(row8, norm[0:1], norm[1:2]) + jnp.zeros((8, 128), F32)
        wire = unit.astype(BF16).astype(F32)
        self.iline[self.z] = wire
        self.send("iline", 4, self.iline.at[self.z], self.line)

    def left(self, unit):
        wire = unit.astype(BF16).astype(F32)
        return jnp.concatenate([wire, unit - wire], axis=0).astype(BF16)

    def against(self, unit, everyone):
        found = lax.dot_general(
            self.left(unit), everyone, (((1,), (1,)), ((), ())), preferred_element_type=F32)
        return folded(found[0:8]), folded(found[8:16])

    def end(self, meanwhile):
        texts = self.tall[...].reshape(512, 128)
        image, image_rest = self.against(self.units[2], texts)
        self.take("iline")
        self.iall[self.own_line] = self.iline[...].reshape(64, 128).astype(BF16)
        self.send("iplane", 5, self.iall.at[self.own_line], self.plane)
        meanwhile()
        self.take("iplane")
        images = self.iall[...].reshape(512, 128)
        text, text_rest = self.against(self.units[0], images)
        kind = lax.broadcasted_iota(jnp.int32, (2, 512), 1) % 8
        mixed = jnp.where(kind < 2, image, jnp.where(
            kind < 4, pltpu.roll(text, 2, 1), jnp.where(
                kind < 6, pltpu.roll(image_rest, 4, 1), pltpu.roll(text_rest, 6, 1))))
        self.dots[self.mp] = stacked(mixed)
        self.send("dots", 6, self.dots.at[self.mp], self.group)
        row = lax.broadcasted_iota(jnp.int32, (8, 128), 0)
        lane = lax.broadcasted_iota(jnp.int32, (8, 128), 1)
        column = (row // 2) * 128 + lane
        kind = column % 8
        place = column // 64
        shard = (place // 2) * 16 + ((column // 8) % 8) * 2 + place % 2
        other = shard * 2 + kind % 2
        own = row % 2
        own_pair = by_parity(row, self.pair_ref[0], self.pair_ref[1])
        match = jnp.where(kind < 2, own_pair, self.pairs[...].astype(jnp.int32)) == jnp.where(
            kind < 2, other, self.dp * 2 + own)
        label = jnp.where(match, 1.0, -1.0)
        scale = jnp.exp(jnp.full((8, 128), self.scale_ref[0], F32))
        self.take("dots")
        dots = self.dots
        dot = ((dots[0] + dots[1]) + dots[2]) + dots[3]
        turned = -label * (scale * dot + self.bias_ref[0])
        small = jnp.exp(-jnp.abs(turned))
        soft = jnp.where(kind < 2, jnp.maximum(turned, 0.0) + jnp.log1p(small), 0.0)
        sigmoid = jnp.where(turned >= 0, 1.0, small) / (1.0 + small)
        slope = jnp.where(kind < 4, -label * sigmoid, 0.0)
        term = scale * slope * (dot + pltpu.roll(dot, 128 - 4, 1))
        loss = parity_sums(soft)
        image_proj = parity_sums(jnp.where(kind < 2, term, 0.0))
        text_proj = parity_sums(jnp.where(kind >= 2, term, 0.0))
        blank = jnp.zeros((2, 512), F32)
        for everyone, kept, proj, at, out in (
            (texts, kind < 2, image_proj, 2, self.emb_ref), (images, kind >= 2, text_proj, 0, self.txt_ref)
        ):
            flat = jnp.where(kept, slope, 0.0)
            flat = jnp.concatenate([flat[2 * q:2 * q + 2] for q in range(4)], axis=1)
            if at == 0:
                flat = pltpu.roll(flat, 512 - 2, 1)
            spread = jnp.concatenate([flat, pltpu.roll(flat, 2, 1), pltpu.roll(flat, 4, 1), blank], axis=0)
            found = jnp.dot(three_terms(spread), everyone, preferred_element_type=F32)
            direction = (found[0:8] + (found[8:16] + found[16:24])) * scale
            grad = (direction - self.units[at] * by_parity(row, proj[0], proj[1])) * self.units[at + 1]
            for b in range(3):
                width = 128 if b < 2 else DL - 256
                out[:, 128 * b:128 * b + width] = grad[2 * b:2 * b + 2, 0:width]
        self.loss_ref[...] = by_parity(lax.broadcasted_iota(jnp.int32, (2, 128), 0), loss[0], loss[1])
        for copies in self.copies.values():
            for copy in copies:
                copy.wait_send()


def tail_scratch():
    dma = pltpu.SemaphoreType.DMA
    pair = lambda n: [dma((n,)), dma((n,))]
    return [
        pltpu.VMEM((4, 2, D), F32), pltpu.VMEM((4, 8, 128), F32), pltpu.VMEM((8, D + 128), F32),
        pltpu.VMEM((4, 8, 128), F32), pltpu.VMEM((8, 8, 128), F32), pltpu.VMEM((8, 8, 128), F32),
        pltpu.VMEM((8, 64, 128), BF16), pltpu.VMEM((8, 64, 128), BF16), pltpu.VMEM((8, 128), F32),
        pltpu.VMEM((4, 8, 128), F32),
    ] + pair(3) + pair(7) + pair(7) + pair(3) + pair(7) + pair(7) + pair(3)


ROWS = 512
MAIN = 1024
TAIL = 64
UNITS = 1076
WINDOW = 5
STAGES = 9
HI = [(1, 0), (1, 1), (2, 0), (2, 1), (0, 0), (0, 1), (3, 0), (4, 1), (5, 1), (6, 0), (6, 1), (7, 1), (8, 0), (8, 1)]
LO = [(3, 1), ('P', 0), ('P', 1), (4, 0), ('P', 2), ('P', 3), (5, 0), (7, 0)]
ORDER = [('F', 1, 0), ('F', 3, 1), ('F', 1, 1), ('F', 2, 0), ('N', 0), ('F', 2, 1), ('e', 0, 0), ('F', 0, 0), ('e', 0, 1), ('F', 0, 1), ('N', 1), ('m', 0), ('F', 3, 0), ('F', 4, 0), ('e', 1, 0), ('e', 1, 1), ('F', 4, 1), ('m', 1), ('H', 0, 0), ('H', 0, 1), ('F', 5, 1), ('N', 2), ('H', 0, 2), ('H', 0, 3), ('F', 6, 0), ('F', 6, 1), ('N', 3), ('H', 0, 4), ('F', 5, 0), ('F', 7, 1), ('E', 1, 0), ('E', 1, 1), ('E', 1, 2), ('F', 7, 0), ('F', 8, 0), ('E', 1, 3), ('M', 1, 0), ('F', 8, 1), ('M', 1, 1), ('H', 1, 0), ('H', 1, 1), ('H', 1, 2), ('H', 1, 3), ('H', 1, 4), ('A', 0, 0), ('A', 0, 1), ('A', 1, 0), ('A', 1, 1), ('B', 0), ('B', 1)]


def main_peers():
    x, z, yh, mp = coords()
    dp = dp_of(x, z, yh)
    return dict(
        core=(dp, mp + 1 - 2 * (mp % 2)),
        lo=(dp, (mp + 2) % 4),
        cross=(dp, 3 - mp),
        hi=(dp + 1 - 2 * (dp % 2), (mp + 2) % 4),
        xp=(dp_of((x + 1) % 4, z, yh), mp),
        xm=(dp_of((x + 3) % 4, z, yh), mp),
        zp=(dp_of(x, (z + 1) % 8, yh), mp),
        zm=(dp_of(x, (z + 7) % 8, yh), mp),
    )


def gelu(u):
    inner = u * (0.7978845608028654 + 0.035677408136300125 * (u * u))
    half = 0.5 * u
    return half + half * jnp.tanh(inner)


def main_kernel(
    patch_ref, inner_ref, outer_ref, text_hbm, counts_hbm, pair_hbm, scale_hbm, bias_hbm,
    loss_ref, emb_ref, txt_ref,
    text_ref, counts_ref, pair_ref, scale_ref, bias_ref, small_sem, w1_own, w2_own, tails, w1_oth, w2_oth, xin, xres, xn, acc, hid, part_out, part_in,
    load_sem, own_sem, patch_send, patch_recv, norm_send, norm_recv, y_send, y_recv,
    side_send, side_recv, part_send, part_recv, heard, *tail_refs,
):
    x, z, yh, mp = coords()
    dp = dp_of(x, z, yh)
    core = mp % 2
    colour = [(x + 2 * z) % 4, (2 * x + z) % 4]
    peers = main_peers()
    barrier = pltpu.get_barrier_semaphore()
    for peer in peers.values():
        pl.semaphore_signal(barrier, inc=1, device_id=peer, device_id_type=MESH)
    smalls = [pltpu.make_async_copy(src, dst, small_sem.at[n]) for n, (src, dst) in enumerate((
        (text_hbm, text_ref), (counts_hbm, counts_ref), (pair_hbm, pair_ref), (scale_hbm, scale_ref),
        (bias_hbm, bias_ref)))]
    loads = [
        pltpu.make_async_copy(inner_ref, w1_own, load_sem.at[0]),
        pltpu.make_async_copy(outer_ref, w2_own, load_sem.at[1]),
    ]
    mine = [
        pltpu.make_async_copy(
            patch_ref.at[:, pl.ds(pl.multiple_of(ROWS * mp + 128 * rb, 128), 128)], xin.at[rb, mp], own_sem.at[rb])
        for rb in range(4)]
    for copy in smalls + mine + loads:
        copy.start()
    tail = Tail(text_ref, counts_ref, pair_ref, scale_ref, bias_ref, loss_ref, emb_ref, txt_ref, *tail_refs)
    smalls[0].wait()
    tail.begin()
    pl.semaphore_wait(barrier, len(peers))

    def patch_copies(rb):
        return [pltpu.make_async_remote_copy(
            src_ref=patch_ref.at[:, pl.ds(pl.multiple_of(ROWS * ((mp + k) % 4) + 128 * rb, 128), 128)],
            dst_ref=xin.at[rb, mp],
            send_sem=patch_send.at[rb, k - 1], recv_sem=patch_recv.at[rb, k - 1],
            device_id=(dp, (mp + k) % 4), device_id_type=MESH) for k in range(1, 4)]

    def place(stage, k):
        if stage == 0:
            rows = pl.ds(pl.multiple_of(colour[k] * 16, 16), 16)
            return tails.at[k, rows], (w1_oth, w2_oth)[k].at[rows]
        src, dst = (inner_ref, w1_oth) if stage < 5 else (outer_ref, w2_oth)
        first = 256 * ((stage - 1) % 4) + 128 * k + colour[k] * 32
        return src.at[pl.ds(pl.multiple_of(first, 32), 32)], dst.at[pl.ds(pl.multiple_of(first + 128, 32), 32)]

    def y_copy(stage, k):
        src, dst = place(stage, k)
        return pltpu.make_async_remote_copy(
            src_ref=src, dst_ref=dst, send_sem=y_send.at[stage, k], recv_sem=y_recv.at[stage, k],
            device_id=peers["hi" if (stage, k) in HI else "lo"], device_id_type=MESH)

    def side_copies(stage, k):
        near, far = (("xp", "xm"), ("zp", "zm")) if k == 0 else (("zp", "zm"), ("xp", "xm"))
        _, at = place(stage, k)
        return [pltpu.make_async_remote_copy(
            src_ref=at, dst_ref=at, send_sem=side_send.at[stage, k, j], recv_sem=side_recv.at[stage, k, j],
            device_id=peers[who], device_id_type=MESH) for j, who in enumerate((near[0], near[1], far[stage % 2]))]

    queues = {"hi": list(HI), "lo": list(LO)}

    def issue(link):
        if queues[link]:
            item = queues[link].pop(0)
            for copy in patch_copies(item[1]) if item[0] == "P" else [y_copy(*item)]:
                copy.start()

    def forward(stage, k):
        copy = y_copy(stage, k)
        copy.wait_recv()
        for side in side_copies(stage, k):
            side.start()
        issue("hi" if (stage, k) in HI else "lo")

    arrived = set()

    def arrive(stage):
        if stage not in arrived:
            arrived.add(stage)
            for k in range(2):
                for copy in side_copies(stage, k):
                    copy.wait_recv()

    def norm_copy(rb):
        at = (rb // 2, (rb % 2) * 2 + core)
        return pltpu.make_async_remote_copy(
            src_ref=xn.at[at], dst_ref=xn.at[at], send_sem=norm_send.at[rb], recv_sem=norm_recv.at[rb],
            device_id=peers["core"], device_id_type=MESH)

    def normalise(rb):
        mine[rb].wait()
        for copy in patch_copies(rb):
            copy.wait_recv()
        issue("lo")
        raw = xin[rb].reshape(D, 128)
        wide = raw.astype(F32)
        wide = wide - jnp.sum(wide, axis=0, keepdims=True) * (1.0 / D)
        spread = jnp.sum(wide * wide, axis=0, keepdims=True) * (1.0 / D)
        xn[rb // 2, (rb % 2) * 2 + core] = (wide * lax.rsqrt(spread + epsilon)).astype(BF16).T
        norm_copy(rb).start()
        xres[rb] = raw.T

    def expand(rows, weights, lo, hi):
        return gelu(lax.dot_general(
            rows, weights[lo:hi, :], (((1,), (1,)), ((), ())), preferred_element_type=F32)).astype(BF16)

    def quarter_expand(rb, n):
        if n == 0:
            norm_copy(rb).wait_recv()
        for j in (2 * n, 2 * n + 1):
            hid[0, 256 * rb:256 * rb + 256, 128 + 256 * j:384 + 256 * j] = expand(
                xn[0, 2 * rb:2 * rb + 2].reshape(256, D), w1_own, 256 * j, 256 * j + 256)

    def quarter_mix(rb):
        acc[0, 2 * rb:2 * rb + 2] = jnp.dot(
            hid[0, 256 * rb:256 * rb + 256, 128:1152], w2_own[0:MAIN, :], preferred_element_type=F32).reshape(2, 128, D)

    def own_expand(half, j):
        if j == 0:
            norm_copy(2 * half).wait_recv()
            norm_copy(2 * half + 1).wait_recv()
        hid[half, :, 128 + 256 * j:384 + 256 * j] = expand(
            xn[half].reshape(512, D), w1_own, 256 * j, 256 * j + 256)

    def mix(half, weights, lo, hi, left, right):
        return jnp.dot(
            hid[half, :, lo:hi], weights[:, left:right], preferred_element_type=F32).reshape(4, 128, right - left)

    def own_mix(half, n):
        left, right = ((0, 640), (640, 1152))[n]
        acc[half, :, :, left:right] = mix(half, w2_own.at[0:MAIN], 128, 1152, left, right)

    def other_expand(half, j):
        arrive(j)
        lo, hi = 256 * j - 128 if j else 0, 256 * j + 128
        hid[half, :, lo:hi] = expand(xn[half].reshape(512, D), w1_oth, lo, hi)

    def other_mix(half, n):
        arrive(5)
        arrive(6)
        left, right = ((0, 640), (640, 1152))[n]
        acc[half, :, :, left:right] += mix(half, w2_oth.at[0:640], 0, 640, left, right)

    def part_copy(rb):
        return pltpu.make_async_remote_copy(
            src_ref=part_out.at[rb], dst_ref=part_in.at[rb], send_sem=part_send.at[rb],
            recv_sem=part_recv.at[rb], device_id=peers["core"], device_id_type=MESH)

    def last_mix(half):
        arrive(7)
        arrive(8)
        acc[half] += mix(half, w2_oth.at[640:1152], 640, 1152, 0, D)
        for r in range(2):
            rb = half * 2 + r
            part_out[rb] = acc[half, 2 * r + 1 - core].astype(BF16)
            part_copy(rb).start()

    tail.greet()
    for _ in range(2):
        issue("hi")
        issue("lo")
    for copy in smalls[1:]:
        copy.wait()
    kept = inner_ref.shape[0] - MAIN
    for k, (own, oth) in enumerate(((w1_own, w1_oth), (w2_own, w2_oth))):
        loads[k].wait()
        value, blank = own[MAIN:MAIN + kept, :], jnp.zeros((TAIL - kept, D), BF16)
        tails[k, 0:kept, :] = value
        tails[k, kept:TAIL, :] = blank
        oth[TAIL:TAIL + kept, :] = value
        oth[TAIL + kept:2 * TAIL, :] = blank
    for _ in range(WINDOW - 2):
        issue("hi")
        issue("lo")
    steps = dict(
        F=forward, N=normalise, e=quarter_expand, m=quarter_mix, E=own_expand, M=own_mix, H=other_expand, A=other_mix, B=last_mix)

    beside = [peers[name] for name in ("lo", "hi", "xp", "xm", "zp", "zm")]

    def tell(n):
        for peer in beside:
            pl.semaphore_signal(heard.at[n], inc=1, device_id=peer, device_id_type=MESH)

    def hear(n):
        pl.semaphore_wait(heard.at[n], len(beside))
        if n < 2:
            tell(n + 1)
    tell(0)
    texts = {4: lambda: hear(0), 8: lambda: hear(1), 12: lambda: (hear(2), tail.text_line()),
             26: tail.text_plane, 48: tail.text_done}
    for at, (name, *where) in enumerate(ORDER):
        steps[name](*where)
        if at in texts:
            texts[at]()

    n0 = counts_ref[0]
    n1 = n0 + counts_ref[1]

    def finish(rb, totals):
        part_copy(rb).wait_recv()
        value = xres[rb].astype(F32) + (acc[rb // 2, (rb % 2) * 2 + core] + part_in[rb].astype(F32))
        shifted = value - jnp.sum(value, axis=1, keepdims=True) * (1.0 / D)
        spread = jnp.sum(shifted * shifted, axis=1, keepdims=True) * (1.0 / D)
        scale = lax.rsqrt(spread + epsilon)
        ids = ROWS * mp + 128 * rb + lax.broadcasted_iota(jnp.int32, (128, 1), 0)
        normed = shifted * scale
        a = jnp.sum(jnp.where(ids < n0, normed, 0.0), axis=0, keepdims=True)
        b = jnp.sum(jnp.where((ids >= n0) & (ids < n1), normed, 0.0), axis=0, keepdims=True)
        return totals[0] + a, totals[1] + b
    zero = jnp.zeros((1, D), F32)
    a, b = lax.fori_loop(0, 4, finish, (zero, zero))
    tail.image_line(a, b)
    tail.image_rows()

    def drain():
        for rb in range(4):
            for copy in patch_copies(rb):
                copy.wait_send()
            norm_copy(rb).wait_send()
            part_copy(rb).wait_send()
        for stage in range(STAGES):
            for k in range(2):
                for copy in [y_copy(stage, k)] + side_copies(stage, k):
                    copy.wait_send()
    tail.end(drain)


def main_scratch():
    dma = pltpu.SemaphoreType.DMA
    return [
        pltpu.VMEM((2, DL), BF16), pltpu.SMEM((2,), jnp.int32), pltpu.SMEM((2,), jnp.int32), pltpu.SMEM((1,), F32),
        pltpu.SMEM((1,), F32), dma((5,)),
        pltpu.VMEM((UNITS, D), BF16), pltpu.VMEM((UNITS, D), BF16), pltpu.VMEM((2, TAIL, D), BF16),
        pltpu.VMEM((D, D), BF16), pltpu.VMEM((D, D), BF16),
        pltpu.VMEM((4, 4, DL, 128), BF16), pltpu.VMEM((4, 128, D), BF16),
        pltpu.VMEM((2, 4, 128, D), BF16), pltpu.VMEM((2, 4, 128, D), F32),
        pltpu.VMEM((2, 512, D), BF16),
        pltpu.VMEM((4, 128, D), BF16), pltpu.VMEM((4, 128, D), BF16),
        dma((2,)), dma((4,)), dma((4, 3)), dma((4, 3)), dma((4,)), dma((4,)), dma((STAGES, 2)), dma((STAGES, 2)),
        dma((STAGES, 2, 3)), dma((STAGES, 2, 3)), dma((4,)), dma((4,)), pltpu.SemaphoreType.REGULAR((3,)),
    ]


def hand_over(loss_ref, emb_ref, txt_ref, loss_out, emb_out, txt_out):
    emb_out[...] = emb_ref[...]
    txt_out[...] = txt_ref[...]
    loss_out[0] = loss_ref[0, 0]
    loss_out[1] = loss_ref[1, 0]


def shards(
    patches, counts, pair_ids, inner_weight, outer_weight, text_embed, log_scale, logit_bias
):
    vmem, smem = pl.BlockSpec(memory_space=pltpu.VMEM), pl.BlockSpec(memory_space=pltpu.SMEM)
    hbm = pl.BlockSpec(memory_space=pl.ANY)
    half = jax.ShapeDtypeStruct((2, DL), F32)
    found = pl.pallas_call(
        main_kernel,
        out_shape=(jax.ShapeDtypeStruct((2, 128), F32), half, half),
        in_specs=[hbm] * 8,
        out_specs=(vmem, vmem, vmem),
        scratch_shapes=main_scratch() + tail_scratch(),
        compiler_params=pltpu.CompilerParams(
            collective_id=1, has_side_effects=True, vmem_limit_bytes=56 * 2**20),
        name="tower",
    )(patches.T, inner_weight.T, outer_weight, text_embed, counts, pair_ids, log_scale, logit_bias)
    return pl.pallas_call(
        hand_over,
        out_shape=(jax.ShapeDtypeStruct((2,), F32), half, half),
        in_specs=[vmem, vmem, vmem],
        out_specs=(smem, vmem, vmem),
        name="hand_over",
    )(*found)


def solution(mesh):
    placed = (
        P("dp", "mp"),
        P("dp"),
        P("dp"),
        P(None, "mp"),
        P("mp", None),
        P("dp", "mp"),
        P(),
        P(),
    )
    return jax.shard_map(
        shards,
        mesh=mesh,
        in_specs=placed,
        out_specs=(P("dp"), P("dp", "mp"), P("dp", "mp")),
        check_vma=False,
    )
```

```python
import functools

import jax
import jax.numpy as jnp
from jax import lax
from jax.experimental import pallas as pl
from jax.experimental.pallas import tpu as pltpu
from jax.sharding import PartitionSpec as P

MESH = pl.DeviceIdType.MESH
epsilon = 1e-06
D = 1152
DL = 288
F32, BF16 = jnp.float32, jnp.bfloat16


def coords():
    dp, mp = lax.axis_index("dp"), lax.axis_index("mp")
    return dp // 16, (dp // 2) % 8, dp % 2, mp


def dp_of(x, z, yh):
    return x * 16 + z * 2 + yh


def tail_peers():
    x, z, yh, mp = coords()
    dp = dp_of(x, z, yh)
    group = [(dp, (mp + k) % 4) for k in range(1, 4)]
    line = [(dp_of(x, (z + k) % 8, yh), mp) for k in range(1, 8)]
    plane = [(dp_of((x + k // 2) % 4, z, (yh + k) % 2), mp) for k in range(1, 8)]
    return group, line, plane


def by_parity(column, even, odd):
    return jnp.where(column % 2 == 0, even, odd)


def parity_sums(values):
    own = jnp.sum(values, axis=1, keepdims=True)
    row = lax.broadcasted_iota(jnp.int32, own.shape, 0)
    even = jnp.sum(jnp.where(row % 2 == 0, own, 0.0), axis=0, keepdims=True)
    odd = jnp.sum(jnp.where(row % 2 == 1, own, 0.0), axis=0, keepdims=True)
    return even, odd


def three_terms(values):
    high = values.astype(BF16).astype(F32)
    rest = values - high
    mid = rest.astype(BF16).astype(F32)
    return jnp.concatenate([high, mid, rest - mid], axis=0).astype(BF16)


def stacked(wide):
    return jnp.concatenate([wide[:, 128 * q:128 * q + 128] for q in range(4)], axis=0)


def folded(dots):
    return dots[0:2] + pltpu.roll(dots, 512 - 2, 1)[2:4] + pltpu.roll(dots, 512 - 4, 1)[4:6]


class Tail:
    def __init__(self, text_ref, counts_ref, pair_ref, scale_ref, bias_ref, loss_ref, emb_ref, txt_ref,
                 psum, tss, wide, units, tline, iline, tall, iall, pairs, dots, *sems):
        self.__dict__.update(locals())
        self.x, self.z, self.yh, self.mp = coords()
        self.dp = dp_of(self.x, self.z, self.yh)
        self.own_line = self.x * 2 + self.yh
        self.group, self.line, self.plane = tail_peers()
        self.copies = {}

    def send(self, name, sem, ref, peers):
        sent, got = self.sems[2 * sem], self.sems[2 * sem + 1]
        self.copies[name] = [pltpu.make_async_remote_copy(
            src_ref=ref, dst_ref=ref, send_sem=sent.at[k], recv_sem=got.at[k],
            device_id=peer, device_id_type=MESH) for k, peer in enumerate(peers)]
        for copy in self.copies[name]:
            copy.start()

    def take(self, name):
        for copy in self.copies[name]:
            copy.wait_recv()

    def begin(self):
        text = self.text_ref[...].astype(F32)
        self.tss[self.mp] = jnp.zeros((8, 128), F32)
        self.tss[self.mp, 0:2, :] = jnp.broadcast_to(jnp.sum(text * text, axis=1, keepdims=True), (2, 128))
        self.units[...] = jnp.zeros((4, 8, 128), F32)
        for b in range(3):
            width = 128 if b < 2 else DL - 256
            self.units[0, 2 * b:2 * b + 2, 0:width] = text[:, 128 * b:128 * b + width]
        self.wide[...] = jnp.zeros((8, D + 128), F32)

    def greet(self):
        self.send("tss", 0, self.tss.at[self.mp], self.group)

    def text_line(self):
        self.take("tss")
        total = ((self.tss[0] + self.tss[1]) + self.tss[2]) + self.tss[3]
        norm = lax.rsqrt(total + epsilon)
        row = lax.broadcasted_iota(jnp.int32, (8, 128), 0)
        norm = by_parity(row, norm[0:1], norm[1:2])
        unit = self.units[0] * norm
        self.units[0] = unit
        self.units[1] = norm
        wire = unit.astype(BF16).astype(F32)
        ids = jnp.where(row == 6, self.pair_ref[0], self.pair_ref[1]).astype(F32)
        self.tline[self.z] = jnp.where(row < 6, wire, ids)
        self.send("tline", 1, self.tline.at[self.z], self.line)

    def text_plane(self):
        self.take("tline")
        self.tall[self.own_line] = self.tline[...].reshape(64, 128).astype(BF16)
        self.send("tplane", 2, self.tall.at[self.own_line], self.plane)

    def text_done(self):
        self.take("tplane")
        first = (lax.broadcasted_iota(jnp.int32, (16, 128), 1) == 0).astype(F32).astype(BF16)
        column = lax.dot_general(
            first, self.tall[...].reshape(512, 128), (((1,), (1,)), ((), ())), preferred_element_type=F32)
        self.pairs[...] = pltpu.roll(stacked(column[0:2]), 128 - 4, 1)

    def image_line(self, first, second):
        self.psum[self.mp, 0:1, :] = first
        self.psum[self.mp, 1:2, :] = second
        self.send("psum", 3, self.psum.at[self.mp], self.group)

    def image_rows(self):
        self.take("psum")
        psum, mp = self.psum, self.mp
        row = lax.broadcasted_iota(jnp.int32, (2, 1), 0)
        count = jnp.where(row == 0, self.counts_ref[0], self.counts_ref[1]).astype(F32)
        pooled = (((psum[0] + psum[1]) + psum[2]) + psum[3]) / count
        norm = lax.rsqrt(jnp.sum(pooled * pooled, axis=1, keepdims=True) + epsilon)
        self.wide[0:2, :D] = pooled * norm
        lane = lax.broadcasted_iota(jnp.int32, (2, 128), 1)
        for b in range(3):
            block = self.wide[0:2, 128 * b:128 * b + 128]
            for k in range(1, 4):
                block = jnp.where(mp == k, self.wide[0:2, DL * k + 128 * b:DL * k + 128 * b + 128], block)
            self.units[2, 2 * b:2 * b + 2, :] = block if b < 2 else jnp.where(lane < DL - 256, block, 0.0)
        row8 = lax.broadcasted_iota(jnp.int32, (8, 128), 0)
        unit = self.units[2]
        self.units[3] = by_parity(row8, norm[0:1], norm[1:2]) + jnp.zeros((8, 128), F32)
        wire = unit.astype(BF16).astype(F32)
        self.iline[self.z] = wire
        self.send("iline", 4, self.iline.at[self.z], self.line)

    def left(self, unit):
        wire = unit.astype(BF16).astype(F32)
        return jnp.concatenate([wire, unit - wire], axis=0).astype(BF16)

    def against(self, unit, everyone):
        found = lax.dot_general(
            self.left(unit), everyone, (((1,), (1,)), ((), ())), preferred_element_type=F32)
        return folded(found[0:8]), folded(found[8:16])

    def end(self, meanwhile):
        texts = self.tall[...].reshape(512, 128)
        image, image_rest = self.against(self.units[2], texts)
        self.take("iline")
        self.iall[self.own_line] = self.iline[...].reshape(64, 128).astype(BF16)
        self.send("iplane", 5, self.iall.at[self.own_line], self.plane)
        meanwhile()
        self.take("iplane")
        images = self.iall[...].reshape(512, 128)
        text, text_rest = self.against(self.units[0], images)
        kind = lax.broadcasted_iota(jnp.int32, (2, 512), 1) % 8
        mixed = jnp.where(kind < 2, image, jnp.where(
            kind < 4, pltpu.roll(text, 2, 1), jnp.where(
                kind < 6, pltpu.roll(image_rest, 4, 1), pltpu.roll(text_rest, 6, 1))))
        self.dots[self.mp] = stacked(mixed)
        self.send("dots", 6, self.dots.at[self.mp], self.group)
        row = lax.broadcasted_iota(jnp.int32, (8, 128), 0)
        lane = lax.broadcasted_iota(jnp.int32, (8, 128), 1)
        column = (row // 2) * 128 + lane
        kind = column % 8
        place = column // 64
        shard = (place // 2) * 16 + ((column // 8) % 8) * 2 + place % 2
        other = shard * 2 + kind % 2
        own = row % 2
        own_pair = by_parity(row, self.pair_ref[0], self.pair_ref[1])
        match = jnp.where(kind < 2, own_pair, self.pairs[...].astype(jnp.int32)) == jnp.where(
            kind < 2, other, self.dp * 2 + own)
        label = jnp.where(match, 1.0, -1.0)
        scale = jnp.exp(jnp.full((8, 128), self.scale_ref[0], F32))
        self.take("dots")
        dots = self.dots
        dot = ((dots[0] + dots[1]) + dots[2]) + dots[3]
        turned = -label * (scale * dot + self.bias_ref[0])
        small = jnp.exp(-jnp.abs(turned))
        soft = jnp.where(kind < 2, jnp.maximum(turned, 0.0) + jnp.log1p(small), 0.0)
        sigmoid = jnp.where(turned >= 0, 1.0, small) / (1.0 + small)
        slope = jnp.where(kind < 4, -label * sigmoid, 0.0)
        term = scale * slope * (dot + pltpu.roll(dot, 128 - 4, 1))
        loss = parity_sums(soft)
        image_proj = parity_sums(jnp.where(kind < 2, term, 0.0))
        text_proj = parity_sums(jnp.where(kind >= 2, term, 0.0))
        blank = jnp.zeros((2, 512), F32)
        for everyone, kept, proj, at, out in (
            (texts, kind < 2, image_proj, 2, self.emb_ref), (images, kind >= 2, text_proj, 0, self.txt_ref)
        ):
            flat = jnp.where(kept, slope, 0.0)
            flat = jnp.concatenate([flat[2 * q:2 * q + 2] for q in range(4)], axis=1)
            if at == 0:
                flat = pltpu.roll(flat, 512 - 2, 1)
            spread = jnp.concatenate([flat, pltpu.roll(flat, 2, 1), pltpu.roll(flat, 4, 1), blank], axis=0)
            found = jnp.dot(three_terms(spread), everyone, preferred_element_type=F32)
            direction = (found[0:8] + (found[8:16] + found[16:24])) * scale
            grad = (direction - self.units[at] * by_parity(row, proj[0], proj[1])) * self.units[at + 1]
            for b in range(3):
                width = 128 if b < 2 else DL - 256
                out[:, 128 * b:128 * b + width] = grad[2 * b:2 * b + 2, 0:width]
        self.loss_ref[...] = by_parity(lax.broadcasted_iota(jnp.int32, (2, 128), 0), loss[0], loss[1])
        for copies in self.copies.values():
            for copy in copies:
                copy.wait_send()


def tail_scratch():
    dma = pltpu.SemaphoreType.DMA
    pair = lambda n: [dma((n,)), dma((n,))]
    return [
        pltpu.VMEM((4, 2, D), F32), pltpu.VMEM((4, 8, 128), F32), pltpu.VMEM((8, D + 128), F32),
        pltpu.VMEM((4, 8, 128), F32), pltpu.VMEM((8, 8, 128), F32), pltpu.VMEM((8, 8, 128), F32),
        pltpu.VMEM((8, 64, 128), BF16), pltpu.VMEM((8, 64, 128), BF16), pltpu.VMEM((8, 128), F32),
        pltpu.VMEM((4, 8, 128), F32),
    ] + pair(3) + pair(7) + pair(7) + pair(3) + pair(7) + pair(7) + pair(3)


ROWS = 512
MAIN = 1024
TAIL = 64
UNITS = 1076
WINDOW = 5
STAGES = 9
HI = [(1, 0), (1, 1), (2, 0), (2, 1), (0, 0), (0, 1), (3, 0), (4, 1), (5, 1), (6, 0), (6, 1), (7, 1), (8, 0), (8, 1)]
LO = [(3, 1), ('P', 0), ('P', 1), (4, 0), ('P', 2), ('P', 3), (5, 0), (7, 0)]
ORDER = [('F', 1, 0), ('F', 3, 1), ('F', 1, 1), ('F', 2, 0), ('N', 0), ('F', 2, 1), ('e', 0, 0), ('F', 0, 0), ('e', 0, 1), ('F', 0, 1), ('N', 1), ('m', 0), ('F', 3, 0), ('F', 4, 0), ('e', 1, 0), ('e', 1, 1), ('F', 4, 1), ('m', 1), ('H', 0, 0), ('H', 0, 1), ('F', 5, 1), ('N', 2), ('H', 0, 2), ('H', 0, 3), ('F', 6, 0), ('F', 6, 1), ('N', 3), ('H', 0, 4), ('F', 5, 0), ('F', 7, 1), ('E', 1, 0), ('E', 1, 1), ('E', 1, 2), ('F', 7, 0), ('F', 8, 0), ('E', 1, 3), ('M', 1, 0), ('F', 8, 1), ('M', 1, 1), ('H', 1, 0), ('H', 1, 1), ('H', 1, 2), ('H', 1, 3), ('H', 1, 4), ('A', 0, 0), ('A', 0, 1), ('A', 1, 0), ('A', 1, 1), ('B', 0), ('B', 1)]


def main_peers():
    x, z, yh, mp = coords()
    dp = dp_of(x, z, yh)
    return dict(
        core=(dp, mp + 1 - 2 * (mp % 2)),
        lo=(dp, (mp + 2) % 4),
        cross=(dp, 3 - mp),
        hi=(dp + 1 - 2 * (dp % 2), (mp + 2) % 4),
        xp=(dp_of((x + 1) % 4, z, yh), mp),
        xm=(dp_of((x + 3) % 4, z, yh), mp),
        zp=(dp_of(x, (z + 1) % 8, yh), mp),
        zm=(dp_of(x, (z + 7) % 8, yh), mp),
    )


def gelu(u):
    inner = u * (0.7978845608028654 + 0.035677408136300125 * (u * u))
    half = 0.5 * u
    return half + half * jnp.tanh(inner)


def main_kernel(
    patch_ref, inner_ref, outer_ref, text_hbm, counts_hbm, pair_hbm, scale_hbm, bias_hbm,
    loss_ref, emb_ref, txt_ref,
    text_ref, counts_ref, pair_ref, scale_ref, bias_ref, small_sem, w1_own, w2_own, tails, w1_oth, w2_oth, xin, xres, xn, acc, hid, part_out, part_in,
    load_sem, own_sem, patch_send, patch_recv, norm_send, norm_recv, y_send, y_recv,
    side_send, side_recv, part_send, part_recv, heard, *tail_refs,
):
    x, z, yh, mp = coords()
    dp = dp_of(x, z, yh)
    core = mp % 2
    colour = [(x + 2 * z) % 4, (2 * x + z) % 4]
    peers = main_peers()
    barrier = pltpu.get_barrier_semaphore()
    for peer in peers.values():
        pl.semaphore_signal(barrier, inc=1, device_id=peer, device_id_type=MESH)
    smalls = [pltpu.make_async_copy(src, dst, small_sem.at[n]) for n, (src, dst) in enumerate((
        (text_hbm, text_ref), (counts_hbm, counts_ref), (pair_hbm, pair_ref), (scale_hbm, scale_ref),
        (bias_hbm, bias_ref)))]
    loads = [
        pltpu.make_async_copy(inner_ref, w1_own, load_sem.at[0]),
        pltpu.make_async_copy(outer_ref, w2_own, load_sem.at[1]),
    ]
    mine = [
        pltpu.make_async_copy(
            patch_ref.at[:, pl.ds(pl.multiple_of(ROWS * mp + 128 * rb, 128), 128)], xin.at[rb, mp], own_sem.at[rb])
        for rb in range(4)]
    for copy in smalls + mine + loads:
        copy.start()
    tail = Tail(text_ref, counts_ref, pair_ref, scale_ref, bias_ref, loss_ref, emb_ref, txt_ref, *tail_refs)
    pl.semaphore_wait(barrier, len(peers))

    def patch_copies(rb):
        return [pltpu.make_async_remote_copy(
            src_ref=patch_ref.at[:, pl.ds(pl.multiple_of(ROWS * ((mp + k) % 4) + 128 * rb, 128), 128)],
            dst_ref=xin.at[rb, mp],
            send_sem=patch_send.at[rb, k - 1], recv_sem=patch_recv.at[rb, k - 1],
            device_id=(dp, (mp + k) % 4), device_id_type=MESH) for k in range(1, 4)]

    def place(stage, k):
        if stage == 0:
            rows = pl.ds(pl.multiple_of(colour[k] * 16, 16), 16)
            return tails.at[k, rows], (w1_oth, w2_oth)[k].at[rows]
        src, dst = (inner_ref, w1_oth) if stage < 5 else (outer_ref, w2_oth)
        first = 256 * ((stage - 1) % 4) + 128 * k + colour[k] * 32
        return src.at[pl.ds(pl.multiple_of(first, 32), 32)], dst.at[pl.ds(pl.multiple_of(first + 128, 32), 32)]

    def y_copy(stage, k):
        src, dst = place(stage, k)
        return pltpu.make_async_remote_copy(
            src_ref=src, dst_ref=dst, send_sem=y_send.at[stage, k], recv_sem=y_recv.at[stage, k],
            device_id=peers["hi" if (stage, k) in HI else "lo"], device_id_type=MESH)

    def side_copies(stage, k):
        near, far = (("xp", "xm"), ("zp", "zm")) if k == 0 else (("zp", "zm"), ("xp", "xm"))
        _, at = place(stage, k)
        return [pltpu.make_async_remote_copy(
            src_ref=at, dst_ref=at, send_sem=side_send.at[stage, k, j], recv_sem=side_recv.at[stage, k, j],
            device_id=peers[who], device_id_type=MESH) for j, who in enumerate((near[0], near[1], far[stage % 2]))]

    queues = {"hi": list(HI), "lo": list(LO)}

    def issue(link):
        if queues[link]:
            item = queues[link].pop(0)
            for copy in patch_copies(item[1]) if item[0] == "P" else [y_copy(*item)]:
                copy.start()

    def forward(stage, k):
        copy = y_copy(stage, k)
        copy.wait_recv()
        for side in side_copies(stage, k):
            side.start()
        issue("hi" if (stage, k) in HI else "lo")

    arrived = set()

    def arrive(stage):
        if stage not in arrived:
            arrived.add(stage)
            for k in range(2):
                for copy in side_copies(stage, k):
                    copy.wait_recv()

    def norm_copy(rb):
        at = (rb // 2, (rb % 2) * 2 + core)
        return pltpu.make_async_remote_copy(
            src_ref=xn.at[at], dst_ref=xn.at[at], send_sem=norm_send.at[rb], recv_sem=norm_recv.at[rb],
            device_id=peers["core"], device_id_type=MESH)

    def normalise(rb):
        mine[rb].wait()
        for copy in patch_copies(rb):
            copy.wait_recv()
        issue("lo")
        raw = xin[rb].reshape(D, 128)
        wide = raw.astype(F32)
        wide = wide - jnp.sum(wide, axis=0, keepdims=True) * (1.0 / D)
        spread = jnp.sum(wide * wide, axis=0, keepdims=True) * (1.0 / D)
        xn[rb // 2, (rb % 2) * 2 + core] = (wide * lax.rsqrt(spread + epsilon)).astype(BF16).T
        norm_copy(rb).start()
        xres[rb] = raw.T

    def expand(rows, weights, lo, hi):
        return gelu(lax.dot_general(
            rows, weights[lo:hi, :], (((1,), (1,)), ((), ())), preferred_element_type=F32)).astype(BF16)

    def quarter_expand(rb, n):
        if n == 0:
            norm_copy(rb).wait_recv()
        for j in (2 * n, 2 * n + 1):
            hid[0, 256 * rb:256 * rb + 256, 128 + 256 * j:384 + 256 * j] = expand(
                xn[0, 2 * rb:2 * rb + 2].reshape(256, D), w1_own, 256 * j, 256 * j + 256)

    def quarter_mix(rb):
        acc[0, 2 * rb:2 * rb + 2] = jnp.dot(
            hid[0, 256 * rb:256 * rb + 256, 128:1152], w2_own[0:MAIN, :], preferred_element_type=F32).reshape(2, 128, D)

    def own_expand(half, j):
        if j == 0:
            norm_copy(2 * half).wait_recv()
            norm_copy(2 * half + 1).wait_recv()
        hid[half, :, 128 + 256 * j:384 + 256 * j] = expand(
            xn[half].reshape(512, D), w1_own, 256 * j, 256 * j + 256)

    def mix(half, weights, lo, hi, left, right):
        return jnp.dot(
            hid[half, :, lo:hi], weights[:, left:right], preferred_element_type=F32).reshape(4, 128, right - left)

    def own_mix(half, n):
        left, right = ((0, 640), (640, 1152))[n]
        acc[half, :, :, left:right] = mix(half, w2_own.at[0:MAIN], 128, 1152, left, right)

    def other_expand(half, j):
        arrive(j)
        lo, hi = 256 * j - 128 if j else 0, 256 * j + 128
        hid[half, :, lo:hi] = expand(xn[half].reshape(512, D), w1_oth, lo, hi)

    def other_mix(half, n):
        arrive(5)
        arrive(6)
        left, right = ((0, 640), (640, 1152))[n]
        acc[half, :, :, left:right] += mix(half, w2_oth.at[0:640], 0, 640, left, right)

    def part_copy(rb):
        return pltpu.make_async_remote_copy(
            src_ref=part_out.at[rb], dst_ref=part_in.at[rb], send_sem=part_send.at[rb],
            recv_sem=part_recv.at[rb], device_id=peers["core"], device_id_type=MESH)

    def last_mix(half):
        arrive(7)
        arrive(8)
        acc[half] += mix(half, w2_oth.at[640:1152], 640, 1152, 0, D)
        for r in range(2):
            rb = half * 2 + r
            part_out[rb] = acc[half, 2 * r + 1 - core].astype(BF16)
            part_copy(rb).start()

    for _ in range(2):
        issue("hi")
        issue("lo")
    smalls[0].wait()
    tail.begin()
    tail.greet()
    for copy in smalls[1:]:
        copy.wait()
    kept = inner_ref.shape[0] - MAIN
    for k, (own, oth) in enumerate(((w1_own, w1_oth), (w2_own, w2_oth))):
        loads[k].wait()
        value, blank = own[MAIN:MAIN + kept, :], jnp.zeros((TAIL - kept, D), BF16)
        tails[k, 0:kept, :] = value
        tails[k, kept:TAIL, :] = blank
        oth[TAIL:TAIL + kept, :] = value
        oth[TAIL + kept:2 * TAIL, :] = blank
    for _ in range(WINDOW - 2):
        issue("hi")
        issue("lo")
    steps = dict(
        F=forward, N=normalise, e=quarter_expand, m=quarter_mix, E=own_expand, M=own_mix, H=other_expand, A=other_mix, B=last_mix)

    beside = [peers[name] for name in ("lo", "hi", "xp", "xm", "zp", "zm")]

    def tell(n):
        for peer in beside:
            pl.semaphore_signal(heard.at[n], inc=1, device_id=peer, device_id_type=MESH)

    def hear(n):
        pl.semaphore_wait(heard.at[n], len(beside))
        if n < 2:
            tell(n + 1)
    tell(0)
    texts = {4: lambda: hear(0), 8: lambda: hear(1), 12: lambda: (hear(2), tail.text_line()),
             26: tail.text_plane, 48: tail.text_done}
    for at, (name, *where) in enumerate(ORDER):
        steps[name](*where)
        if at in texts:
            texts[at]()

    n0 = counts_ref[0]
    n1 = n0 + counts_ref[1]

    def finish(rb, totals):
        part_copy(rb).wait_recv()
        value = xres[rb].astype(F32) + (acc[rb // 2, (rb % 2) * 2 + core] + part_in[rb].astype(F32))
        shifted = value - jnp.sum(value, axis=1, keepdims=True) * (1.0 / D)
        spread = jnp.sum(shifted * shifted, axis=1, keepdims=True) * (1.0 / D)
        scale = lax.rsqrt(spread + epsilon)
        ids = ROWS * mp + 128 * rb + lax.broadcasted_iota(jnp.int32, (128, 1), 0)
        normed = shifted * scale
        a = jnp.sum(jnp.where(ids < n0, normed, 0.0), axis=0, keepdims=True)
        b = jnp.sum(jnp.where((ids >= n0) & (ids < n1), normed, 0.0), axis=0, keepdims=True)
        return totals[0] + a, totals[1] + b
    zero = jnp.zeros((1, D), F32)
    a, b = lax.fori_loop(0, 4, finish, (zero, zero))
    tail.image_line(a, b)
    tail.image_rows()

    def drain():
        for rb in range(4):
            for copy in patch_copies(rb):
                copy.wait_send()
            norm_copy(rb).wait_send()
            part_copy(rb).wait_send()
        for stage in range(STAGES):
            for k in range(2):
                for copy in [y_copy(stage, k)] + side_copies(stage, k):
                    copy.wait_send()
    tail.end(drain)


def main_scratch():
    dma = pltpu.SemaphoreType.DMA
    return [
        pltpu.VMEM((2, DL), BF16), pltpu.SMEM((2,), jnp.int32), pltpu.SMEM((2,), jnp.int32), pltpu.SMEM((1,), F32),
        pltpu.SMEM((1,), F32), dma((5,)),
        pltpu.VMEM((UNITS, D), BF16), pltpu.VMEM((UNITS, D), BF16), pltpu.VMEM((2, TAIL, D), BF16),
        pltpu.VMEM((D, D), BF16), pltpu.VMEM((D, D), BF16),
        pltpu.VMEM((4, 4, DL, 128), BF16), pltpu.VMEM((4, 128, D), BF16),
        pltpu.VMEM((2, 4, 128, D), BF16), pltpu.VMEM((2, 4, 128, D), F32),
        pltpu.VMEM((2, 512, D), BF16),
        pltpu.VMEM((4, 128, D), BF16), pltpu.VMEM((4, 128, D), BF16),
        dma((2,)), dma((4,)), dma((4, 3)), dma((4, 3)), dma((4,)), dma((4,)), dma((STAGES, 2)), dma((STAGES, 2)),
        dma((STAGES, 2, 3)), dma((STAGES, 2, 3)), dma((4,)), dma((4,)), pltpu.SemaphoreType.REGULAR((3,)),
    ]


def hand_over(loss_ref, emb_ref, txt_ref, loss_out, emb_out, txt_out):
    emb_out[...] = emb_ref[...]
    txt_out[...] = txt_ref[...]
    loss_out[0] = loss_ref[0, 0]
    loss_out[1] = loss_ref[1, 0]


def shards(
    patches, counts, pair_ids, inner_weight, outer_weight, text_embed, log_scale, logit_bias
):
    vmem, smem = pl.BlockSpec(memory_space=pltpu.VMEM), pl.BlockSpec(memory_space=pltpu.SMEM)
    hbm = pl.BlockSpec(memory_space=pl.ANY)
    half = jax.ShapeDtypeStruct((2, DL), F32)
    found = pl.pallas_call(
        main_kernel,
        out_shape=(jax.ShapeDtypeStruct((2, 128), F32), half, half),
        in_specs=[hbm] * 8,
        out_specs=(vmem, vmem, vmem),
        scratch_shapes=main_scratch() + tail_scratch(),
        compiler_params=pltpu.CompilerParams(
            collective_id=1, has_side_effects=True, vmem_limit_bytes=56 * 2**20),
        name="tower",
    )(patches.T, inner_weight.T, outer_weight, text_embed, counts, pair_ids, log_scale, logit_bias)
    return pl.pallas_call(
        hand_over,
        out_shape=(jax.ShapeDtypeStruct((2,), F32), half, half),
        in_specs=[vmem, vmem, vmem],
        out_specs=(smem, vmem, vmem),
        name="hand_over",
    )(*found)


def solution(mesh):
    placed = (
        P("dp", "mp"),
        P("dp"),
        P("dp"),
        P(None, "mp"),
        P("mp", None),
        P("dp", "mp"),
        P(),
        P(),
    )
    return jax.shard_map(
        shards,
        mesh=mesh,
        in_specs=placed,
        out_specs=(P("dp"), P("dp", "mp"), P("dp", "mp")),
        check_vma=False,
    )
```
